128 devices in a mesh: rep: 16 (over z, x), row: 8 (over y, core).
Axes of the slice: x: 4, y: 4, z: 4, core: 2. Of those that a mesh axis runs over, the one named last changes fastest.
Arguments:
- delta: bfloat16 [16, 896, 28672], P('rep', 'row')
- error: bfloat16 [16, 896, 28672], P('rep', 'row'), may hold values from -2 to 2
- steps: int32 [16], P('rep'), may hold values from 16 to 64
- q_start: bfloat16 [28672, 64], replicated, may hold values from -0.03125 to 0.03125
- params: float32 [896, 28672], P('row', 'rep'), may hold values from -6 to 6
- momentum: float32 [896, 28672], P('row', 'rep'), may hold values from -2 to 2
Outputs:
- params_new: float32 [896, 28672], P('row', 'rep')
- momentum_new: float32 [896, 28672], P('row', 'rep')
- error_new: bfloat16 [16, 896, 28672], P('rep', 'row')
The draws below stay inside these ranges and needn't reach their ends.
All inputs are finite; a program needn't handle non-finite values.
Results may differ from the reference program's by a relative error of at most 0.001.
Values sent between devices are 32-bit elements; how exact they have to be, the bound alone decides.
No kernel may reach another device: no remote copies, remote signals or barrier semaphores. Data moves between devices by JAX's collectives and lax.ppermute only.
A program may use at most 128 MiB of HBM per device.

```python
import jax
import jax.numpy as jnp
from jax import lax

FF = 28672
RANK = 64
ROWS = 896
REPS = 16


def draw_delta(key, part):
    key = jax.random.fold_in(key, 1)
    keys = jax.random.split(key, 2)
    common = jax.random.normal(keys[0], (ROWS, FF), jnp.float32)
    own = jax.random.normal(keys[1], (REPS, ROWS, FF), jnp.float32)
    values = 0.8 * common[None] + 0.6 * own
    return values.astype(jnp.bfloat16)


def draw_steps(key, part):
    key = jax.random.fold_in(key, 2)
    base = jax.random.randint(key, (REPS,), 16, 33)
    ramp = 32 * jnp.arange(REPS, dtype=jnp.int32) // max(REPS - 1, 1)
    counts = (base + ramp).astype(jnp.int32)
    return counts.at[REPS - 1].set(64).astype(jnp.int32)


def levels(stream_key, dims, cuts, least, largest):
    factor_of = 1.0
    for position, parts in cuts:
        heights = jax.random.uniform(jax.random.fold_in(jax.random.fold_in(stream_key, 6), position), (parts,), jnp.float32, least / len(cuts), largest / len(cuts))
        factor_of = factor_of * jnp.repeat(jnp.exp(heights), dims[position] // parts).reshape((-1,) + (1,) * (len(dims) - 1 - position))
    return factor_of


def noise(stream_key, shape, spread, reach, cuts=(), held_as=jnp.bfloat16):
    array = spread * jax.random.normal(stream_key, shape, jnp.float32)
    if cuts:
        array = array * levels(stream_key, shape, cuts, -0.22, 0.18)
    return jnp.clip(array, -reach, reach).astype(held_as)


def setup_inputs(seed: int = 0) -> dict:
    key_of = jax.random.split(jax.random.key(seed), 7)
    return {
        "delta": draw_delta(jax.random.fold_in(key_of[6], 71), 0),
        "error": noise(key_of[1], (REPS, ROWS, FF), 0.3, 2.0, ((0, 16), (1, 8))),
        "steps": draw_steps(jax.random.fold_in(key_of[6], 71), 0),
        "q_start": noise(key_of[3], (FF, RANK), FF ** -0.5, 0.03125),
        "params": noise(key_of[4], (ROWS, FF), 1.0, 6.0, ((0, 8), (1, 16)), jnp.float32),
        "momentum": noise(key_of[5], (ROWS, FF), 0.3, 2.0, ((0, 8), (1, 16)), jnp.float32),
    }


outer_lr = 0.7
beta = 0.9

def reference(delta, error, steps, q_start, params, momentum):
    highest = lax.Precision.HIGHEST
    weights = steps.astype(jnp.float32)
    total = jnp.sum(weights)
    q_wide = q_start.astype(jnp.float32)
    rank = q_start.shape[1]
    rows = delta.shape[1]
    width = delta.shape[2]

    def p_step(acc, inputs):
        part_delta, part_error, weight = inputs
        merged = part_delta.astype(jnp.float32) + part_error.astype(jnp.float32)
        return (acc + weight * jnp.dot(merged, q_wide, precision=highest), None)
    p_sum, _ = lax.scan(p_step, jnp.zeros((rows, rank), jnp.float32), (delta, error, weights))
    gram = jnp.dot(p_sum.T, p_sum, precision=highest)
    lower = jnp.linalg.cholesky(gram)
    p_hat = jax.scipy.linalg.solve_triangular(lower, p_sum.T, lower=True).T

    def q_step(acc, inputs):
        part_delta, part_error, weight = inputs
        merged = part_delta.astype(jnp.float32) + part_error.astype(jnp.float32)
        term = lax.dot_general(merged, p_hat, (((0,), (0,)), ((), ())), precision=highest)
        return (acc + weight * term, None)
    q_acc, _ = lax.scan(q_step, jnp.zeros((width, rank), jnp.float32), (delta, error, weights))
    q_new = q_acc / total
    approx = lax.dot_general(p_hat, q_new, (((1,), (1,)), ((), ())), precision=highest)

    def new_error(inputs):
        part_delta, part_error = inputs
        merged = part_delta.astype(jnp.float32) + part_error.astype(jnp.float32)
        return (merged - approx).astype(jnp.bfloat16)
    error_new = lax.map(new_error, (delta, error))
    momentum_new = beta * momentum + approx
    params_new = params - outer_lr * (approx + beta * momentum_new)
    return (params_new, momentum_new, error_new)
```

```python
import functools

import jax
import jax.numpy as jnp
from jax import lax
from jax.experimental import pallas as pl
from jax.experimental.pallas import tpu as pltpu
from jax.sharding import Mesh, PartitionSpec as P

outer_lr = 0.7
beta = 0.9

AXES = ("zh", "zl", "xh", "xl", "yh", "yl", "c")
REP = ("zh", "zl", "xh", "xl")
ROW = ("yh", "yl", "c")
HIGH = ("zh", "xh", "yh")
ROUTES = (("xl", "yl", "zl"), ("yl", "zl", "xl"), ("zl", "xl", "yl"))

TILES = 7
WIDE = TILES * 128
COUNTS = (5, 5, 6)
FIRST = (0, 5, 10)
HALF = 16
BF = jnp.bfloat16
F32 = jnp.float32
VMEM_LIMIT = 48 << 20


def params_of(**kw):
    return pltpu.CompilerParams(vmem_limit_bytes=VMEM_LIMIT, **kw)


def turn(x, axes, step):
    return lax.ppermute(x, axes, [(i, (i + step) % 4) for i in range(4)])


def swap(x, axis):
    return lax.ppermute(x, axis, [(0, 1), (1, 0)])


def p_kernel(steps_ref, d_ref, e_ref, q_ref, out_ref, acc_ref):
    i = pl.program_id(0)

    @pl.when(i == 0)
    def _():
        acc_ref[...] = jnp.zeros_like(acc_ref)

    both = jnp.concatenate([d_ref[0], e_ref[0]], axis=0)
    acc_ref[...] += lax.dot_general(both, q_ref[...], (((1,), (1,)), ((), ())), preferred_element_type=F32)

    @pl.when(i == pl.num_programs(0) - 1)
    def _():
        count = steps_ref[0].astype(F32)
        out_ref[...] = jnp.full(out_ref.shape, count, F32)
        out_ref[0:112, 0:64] = count * (acc_ref[0:112, :] + acc_ref[112:224, :])


def left_factor(delta, error, q_t, steps):
    width = delta.shape[2]
    block = 2048
    return pl.pallas_call(
        p_kernel,
        grid=(width // block,),
        in_specs=[
            pl.BlockSpec(memory_space=pltpu.SMEM),
            pl.BlockSpec((1, 112, block), lambda i: (0, 0, i)),
            pl.BlockSpec((1, 112, block), lambda i: (0, 0, i)),
            pl.BlockSpec((64, block), lambda i: (0, i)),
        ],
        out_specs=pl.BlockSpec((120, 128), lambda i: (0, 0)),
        out_shape=jax.ShapeDtypeStruct((120, 128), F32),
        scratch_shapes=[pltpu.VMEM((224, 64), F32)],
        compiler_params=params_of(),
        name="left_factor",
    )(steps, delta, error, q_t)


def prep_kernel(steps_ref, a_ref, b_ref, c_ref, d_ref, p_ref, lhs_ref, gram_ref):
    both = (a_ref[...] + b_ref[...]) + (c_ref[...] + d_ref[...])
    p = both[0:112, 0:64]
    total = both[112:113, 0:1]
    p_ref[...] = both
    top = jnp.max(jnp.abs(p), axis=0, keepdims=True)
    weight = steps_ref[0].astype(F32) / total
    unit = p * (1.0 / jnp.maximum(top, 1e-37)) * weight
    flat = unit.T
    high = flat.astype(BF).astype(F32)
    low = flat - high
    lhs_ref[0:64, :] = jnp.concatenate([high, high], axis=1).astype(BF)
    lhs_ref[64:128, :] = jnp.concatenate([low, low], axis=1).astype(BF)
    gram_ref[...] = jnp.zeros_like(gram_ref)
    gram_ref[0:64, 0:64] = lax.dot_general(p, p, (((0,), (0,)), ((), ())), precision=lax.Precision.HIGHEST, preferred_element_type=F32)
    gram_ref[64:65, 0:64] = top


def prepare(steps, a, b, c, d):
    vm = pl.BlockSpec(memory_space=pltpu.VMEM)
    return pl.pallas_call(
        prep_kernel,
        in_specs=[pl.BlockSpec(memory_space=pltpu.SMEM), vm, vm, vm, vm],
        out_specs=[vm, vm, vm],
        out_shape=[
            jax.ShapeDtypeStruct((120, 128), F32),
            jax.ShapeDtypeStruct((128, 224), BF),
            jax.ShapeDtypeStruct((72, 128), F32),
        ],
        compiler_params=params_of(),
        name="prepare",
    )(steps, a, b, c, d)


def product(lhs_ref, d_ref, e_ref):
    both = jnp.concatenate([d_ref[0], e_ref[0]], axis=0)
    r = lax.dot_general(lhs_ref[...], both, (((1,), (0,)), ((), ())), preferred_element_type=F32)
    return r[0:64] + r[64:128]


def send_kernel(s_ref, lhs_ref, d_ref, e_ref, out_ref):
    v = product(lhs_ref, d_ref, e_ref)
    for i in range(8):
        for t in range(TILES):
            out_ref[i, t] = v[8 * i:8 * i + 8, 128 * t:128 * t + 128]


def q_send(where, lhs, delta, error, k):
    n, first = COUNTS[k], FIRST[k]
    column = lambda i, s: (0, 0, (1 - s[0]) * HALF + first + i)
    return pl.pallas_call(
        send_kernel,
        grid_spec=pltpu.PrefetchScalarGridSpec(
            num_scalar_prefetch=1,
            grid=(n,),
            in_specs=[
                pl.BlockSpec((128, 224), lambda i, s: (0, 0)),
                pl.BlockSpec((1, 112, WIDE), column),
                pl.BlockSpec((1, 112, WIDE), column),
            ],
            out_specs=pl.BlockSpec((8, TILES, 8, 128), lambda i, s: (0, i, 0, 0)),
        ),
        out_shape=jax.ShapeDtypeStruct((8, n * TILES, 8, 128), F32),
        compiler_params=params_of(),
        cost_estimate=pl.CostEstimate(flops=2 * 128 * 224 * n * WIDE, bytes_accessed=n * WIDE * (448 + 256), transcendentals=0),
        name="q_send",
    )(where, lhs, delta, error)


def keep_kernel(s_ref, lhs_ref, d_ref, e_ref, r_ref, own_ref, other_ref, keep_ref, send_ref, scr_ref):
    v = product(lhs_ref, d_ref, e_ref)
    for i in range(8):
        own = own_ref[8 * i:8 * i + 8, :]
        other = other_ref[8 * i:8 * i + 8, :]
        for t in range(TILES):
            scr_ref[i, t] = own * v[8 * i:8 * i + 8, 128 * t:128 * t + 128] + other * r_ref[i, t]
    bit = s_ref[1]
    keep_ref[...] = scr_ref[pl.ds(bit * 4, 4)]
    send_ref[...] = scr_ref[pl.ds((1 - bit) * 4, 4)]


def q_keep(where, lhs, delta, error, arrived, own, other, k):
    n, first = COUNTS[k], FIRST[k]
    column = lambda i, s: (0, 0, s[0] * HALF + first + i)
    fixed = lambda i, s: (0, 0)
    moving = lambda i, s: (0, i, 0, 0)
    half = jax.ShapeDtypeStruct((4, n * TILES, 8, 128), F32)
    return pl.pallas_call(
        keep_kernel,
        grid_spec=pltpu.PrefetchScalarGridSpec(
            num_scalar_prefetch=1,
            grid=(n,),
            in_specs=[
                pl.BlockSpec((128, 224), fixed),
                pl.BlockSpec((1, 112, WIDE), column),
                pl.BlockSpec((1, 112, WIDE), column),
                pl.BlockSpec((8, TILES, 8, 128), moving),
                pl.BlockSpec((64, 128), fixed),
                pl.BlockSpec((64, 128), fixed),
            ],
            out_specs=[pl.BlockSpec((4, TILES, 8, 128), moving)] * 2,
            scratch_shapes=[pltpu.VMEM((8, TILES, 8, 128), F32)],
        ),
        out_shape=[half, half],
        compiler_params=params_of(),
        cost_estimate=pl.CostEstimate(flops=2 * 128 * 224 * n * WIDE, bytes_accessed=n * WIDE * (448 + 512), transcendentals=0),
        name="q_keep",
    )(where, lhs, delta, error, arrived, own, other)


def approx_of(bit, w_ref, a_ref, b_ref, scr_ref):
    for i in range(4):
        for t in range(TILES):
            scr_ref[pl.ds((bit * 4 + i) * 8, 8), 128 * t:128 * t + 128] = a_ref[i, t]
            scr_ref[pl.ds(((1 - bit) * 4 + i) * 8, 8), 128 * t:128 * t + 128] = b_ref[i, t]
    q = scr_ref[...]
    high = q.astype(BF)
    low = (q - high.astype(F32)).astype(BF)
    rhs = jnp.concatenate([high, low, high], axis=0)
    return lax.dot_general(w_ref[...], rhs, (((1,), (0,)), ((), ())), preferred_element_type=F32)


def error_kernel(s_ref, w_ref, a_ref, b_ref, d_ref, e_ref, *rest):
    out_ref, scr_ref = rest[-2], rest[-1]
    approx = approx_of(s_ref[1], w_ref, a_ref, b_ref, scr_ref)
    out_ref[0] = ((d_ref[0].astype(F32) + e_ref[0].astype(F32)) - approx).astype(BF)


def new_error(where, w, a, b, delta, error, base, k):
    n, first = COUNTS[k], FIRST[k]
    column = lambda i, s: (0, 0, s[0] * HALF + first + i)
    moving = lambda i, s: (0, i, 0, 0)
    specs = [
        pl.BlockSpec((112, 192), lambda i, s: (0, 0)),
        pl.BlockSpec((4, TILES, 8, 128), moving),
        pl.BlockSpec((4, TILES, 8, 128), moving),
        pl.BlockSpec((1, 112, WIDE), column),
        pl.BlockSpec((1, 112, WIDE), column),
    ]
    args = [where, w, a, b, delta, error]
    aliases = {}
    if base is not None:
        specs.append(pl.BlockSpec(memory_space=pl.ANY))
        args.append(base)
        aliases = {6: 0}
    return pl.pallas_call(
        error_kernel,
        grid_spec=pltpu.PrefetchScalarGridSpec(
            num_scalar_prefetch=1,
            grid=(n,),
            in_specs=specs,
            out_specs=pl.BlockSpec((1, 112, WIDE), column),
            scratch_shapes=[pltpu.VMEM((64, WIDE), F32)],
        ),
        out_shape=jax.ShapeDtypeStruct(delta.shape, BF),
        input_output_aliases=aliases,
        compiler_params=params_of(),
        cost_estimate=pl.CostEstimate(flops=2 * 112 * 192 * n * WIDE, bytes_accessed=n * WIDE * (672 + 256), transcendentals=0),
        name="new_error",
    )(*args)


def outer_kernel(s_ref, w_ref, *refs):
    sources = refs[0:12]
    par_ref, mom_ref, np_ref, nm_ref, a_ref, b_ref, scr_ref, sem = refs[12:]
    core = s_ref[0]
    for j in range(2):
        block = 2 * s_ref[4] + j
        for side in range(2):
            for k in range(3):
                first = side * HALF + FIRST[k]
                here = (block >= first) & (block < first + COUNTS[k])
                for own in range(2):
                    a_src, b_src = sources[(own * 3 + k) * 2], sources[(own * 3 + k) * 2 + 1]

                    @pl.when(here & (core == (side if own == 0 else 1 - side)))
                    def _():
                        tiles = pl.ds((block - first) * TILES, TILES)
                        one = pltpu.make_async_copy(a_src.at[:, tiles], a_ref.at[j, 0], sem.at[j, 0])
                        two = pltpu.make_async_copy(b_src.at[:, tiles], b_ref.at[j, 0], sem.at[j, 1])
                        one.start()
                        two.start()
                        one.wait()
                        two.wait()
    for j in range(2):
        block = 2 * s_ref[4] + j
        inner = lax.rem(block, HALF)
        bit = jnp.where(inner < FIRST[1], s_ref[1], jnp.where(inner < FIRST[2], s_ref[2], s_ref[3]))
        approx = approx_of(bit, w_ref, a_ref.at[j, 0], b_ref.at[j, 0], scr_ref)
        lanes = slice(j * WIDE, (j + 1) * WIDE)
        momentum = beta * mom_ref[:, lanes] + approx
        nm_ref[:, lanes] = momentum
        np_ref[:, lanes] = par_ref[:, lanes] - outer_lr * (approx + beta * momentum)


def outer_update(where, w, sources, params, momentum):
    vm = pl.BlockSpec(memory_space=pltpu.VMEM)
    shape = jax.ShapeDtypeStruct(params.shape, F32)
    return pl.pallas_call(
        outer_kernel,
        in_specs=[pl.BlockSpec(memory_space=pltpu.SMEM), vm] + [pl.BlockSpec(memory_space=pl.ANY)] * 12 + [vm, vm],
        out_specs=[vm, vm],
        out_shape=[shape, shape],
        scratch_shapes=[
            pltpu.VMEM((2, 1, 4, TILES, 8, 128), F32),
            pltpu.VMEM((2, 1, 4, TILES, 8, 128), F32),
            pltpu.VMEM((64, WIDE), F32),
            pltpu.SemaphoreType.DMA((2, 2)),
        ],
        compiler_params=params_of(),
        name="outer_update",
    )(where, w, *sources, params, momentum)


def local(delta, error, steps, q_start, params, momentum):
    highest = lax.Precision.HIGHEST
    bit = {a: lax.axis_index(a) for a in AXES}
    core = bit["c"]
    rep = lax.axis_index(REP)

    own = left_factor(delta, error, q_start.T, steps)
    X, Z = ("xh", "xl"), ("zh", "zl")
    own = (own + turn(own, X, 2)) + (turn(own, X, 1) + turn(own, X, 3))
    p_all, lhs, gram_own = prepare(steps, own, turn(own, Z, 2), turn(own, Z, 1), turn(own, Z, 3))

    gram_near = swap(gram_own, "c")
    top_own, top_near = gram_own[64, :64], gram_near[64, :64]
    row64 = lax.broadcasted_iota(jnp.int32, gram_own.shape, 0) == 64
    join = lambda a, b: jnp.where(row64, jnp.maximum(a, b), a + b)
    both = join(gram_own, gram_near)
    Y = ("yh", "yl")
    both = join(join(both, turn(both, Y, 2)), join(turn(both, Y, 1), turn(both, Y, 3)))
    gram, top = both[:64, :64], both[64, :64]
    scale_own = jnp.broadcast_to((top_own / top)[:, None], (64, 128))
    scale_near = jnp.broadcast_to((top_near / top)[:, None], (64, 128))

    wheres = [jnp.stack([core, bit[r[0]]]) for r in ROUTES]
    arrived = [swap(q_send(wheres[k], lhs, delta, error, k), "c") for k in range(3)]
    parts = []
    for k, (d0, d1, d2) in enumerate(ROUTES):
        keep, send = q_keep(wheres[k], lhs, delta, error, arrived[k], scale_own, scale_near, k)
        got = swap(send, d0)
        for d in (d1, d2):
            n = keep.shape[0] // 2
            take = lambda x, b: lax.dynamic_slice_in_dim(x, b * n, n, 0)
            send = take(keep, 1 - bit[d]) + take(got, 1 - bit[d])
            keep = take(keep, bit[d]) + take(got, bit[d])
            got = swap(send, d)
        parts.append(keep[0] + got[0])
    mine = jnp.concatenate(parts, axis=0)
    mine = lax.all_to_all(mine, HIGH, 0, 0, tiled=True)
    mine = jnp.sum(mine.reshape(8, 2 * TILES, 8, 128), axis=0)

    inv_top = 1.0 / top
    lower = jnp.linalg.cholesky(gram * inv_top[:, None] * inv_top[None, :])
    inverse = jax.scipy.linalg.solve_triangular(lower, jnp.eye(64, dtype=F32), lower=True)
    p_hat = jnp.dot(p_all[:112, :64] * inv_top[None, :], inverse.T, precision=highest)
    w = jnp.dot(p_hat, inverse, precision=highest)
    w_high = w.astype(BF).astype(F32)
    w_cat = jnp.concatenate([w_high, w_high, w - w_high], axis=1).astype(BF)

    full = lax.all_gather(mine, HIGH, axis=0, tiled=True)
    sides = []
    for k, (d0, d1, d2) in enumerate(ROUTES):
        v = full[FIRST[k] * TILES:(FIRST[k] + COUNTS[k]) * TILES][None]
        for d in (d2, d1):
            got = swap(v, d)
            v = jnp.where(bit[d] == 0, jnp.concatenate([v, got], 0), jnp.concatenate([got, v], 0))
        sides.append((v, swap(v, d0)))
    error_new = None
    for k in range(3):
        error_new = new_error(wheres[k], w_cat, *sides[k], delta, error, error_new, k)
    far = [(swap(a, "c"), swap(b, "c")) for a, b in sides]
    for k in range(3):
        flipped = jnp.stack([1 - core, bit[ROUTES[k][0]]])
        error_new = new_error(flipped, w_cat, *far[k], delta, error, error_new, k)
    sources = [x for pair in sides + far for x in pair]
    where = jnp.stack([core] + [bit[r[0]] for r in ROUTES] + [rep])
    params_new, momentum_new = outer_update(where, w_cat, sources, params, momentum)
    return (params_new, momentum_new, error_new)


def solution(mesh):
    fine = Mesh(mesh.devices.reshape((2,) * 7), AXES)
    in_specs = (
        P(REP, ROW, None),
        P(REP, ROW, None),
        P(REP),
        P(),
        P(ROW, REP),
        P(ROW, REP),
    )
    out_specs = (P(ROW, REP), P(ROW, REP), P(REP, ROW, None))
    return jax.shard_map(local, mesh=fine, in_specs=in_specs, out_specs=out_specs, check_vma=False)
```

```python
import jax
import jax.numpy as jnp
from jax import lax
from jax.experimental import pallas as pl
from jax.experimental.pallas import tpu as pltpu
from jax.sharding import Mesh, PartitionSpec as P

outer_lr = 0.7
beta = 0.9

AXES = ("z", "x", "y", "c")
REP = ("z", "x")
ROW = ("y", "c")
ROUTES = (("x", "y", "z"), ("y", "z", "x"), ("z", "x", "y"))

HALF = 112
COUNTS = (37, 37, 38)
FIRST = (0, 37, 74)
BF = jnp.bfloat16
F32 = jnp.float32
HBM = pl.BlockSpec(memory_space=pltpu.HBM)
ANY = pl.BlockSpec(memory_space=pl.ANY)
VM = pl.BlockSpec(memory_space=pltpu.VMEM)
SM = pl.BlockSpec(memory_space=pltpu.SMEM)
DMA = pltpu.SemaphoreType.DMA


def params_of(mib=58):
    return pltpu.CompilerParams(vmem_limit_bytes=mib << 20)


def turn(x, axis, step):
    return lax.ppermute(x, axis, [(i, (i + step) % 4) for i in range(4)])


def low(x, axis):
    return lax.ppermute(x, axis, [(i, i ^ 1) for i in range(4)])


def high(x, axis):
    return lax.ppermute(x, axis, [(i, 3 - i) for i in range(4)])


def swap(x):
    return lax.ppermute(x, "c", [(0, 1), (1, 0)])


def start(src, dst, sem):
    copy = pltpu.make_async_copy(src, dst, sem)
    copy.start()
    return copy


P_BLOCK = 4096


def p_kernel(steps_ref, d_ref, e_ref, q_ref, out_ref, both_ref, qb_ref, sem):
    n = d_ref.shape[2] // P_BLOCK
    copies = []
    for i in range(n):
        cols = slice(i * P_BLOCK, (i + 1) * P_BLOCK)
        copies.append((
            start(d_ref.at[0, :, cols], both_ref.at[0:112, cols], sem.at[i, 0]),
            start(e_ref.at[0, :, cols], both_ref.at[112:224, cols], sem.at[i, 1]),
            start(q_ref.at[:, cols], qb_ref.at[:, cols], sem.at[i, 2]),
        ))
    acc_d = jnp.zeros((112, 64), F32)
    acc_e = jnp.zeros((112, 64), F32)
    dims = (((1,), (1,)), ((), ()))
    for i in range(n):
        cols = slice(i * P_BLOCK, (i + 1) * P_BLOCK)
        for copy in copies[i]:
            copy.wait()
        acc_d = acc_d + lax.dot_general(both_ref[0:112, cols], qb_ref[:, cols], dims, preferred_element_type=F32)
        acc_e = acc_e + lax.dot_general(both_ref[112:224, cols], qb_ref[:, cols], dims, preferred_element_type=F32)
    count = steps_ref[0].astype(F32)
    p = count * (acc_d + acc_e)
    out_ref[56:64, :] = jnp.full((8, 128), count, F32)
    out_ref[0:56, :] = jnp.concatenate([p[0:56], p[56:112]], axis=1)


def left_factor(delta, error, q_t, steps):
    width = delta.shape[2]
    return pl.pallas_call(
        p_kernel,
        in_specs=[SM, HBM, HBM, HBM],
        out_specs=VM,
        out_shape=jax.ShapeDtypeStruct((64, 128), F32),
        scratch_shapes=[
            pltpu.VMEM((224, width), BF),
            pltpu.VMEM((64, width), BF),
            DMA((width // P_BLOCK, 3)),
        ],
        compiler_params=params_of(),
        name="left_factor",
    )(steps, delta, error, q_t)


def prep_kernel(steps_ref, a_ref, b_ref, c_ref, d_ref, p_ref, lhs_ref, gram_ref):
    both = (a_ref[...] + b_ref[...]) + (c_ref[...] + d_ref[...])
    p = jnp.concatenate([both[0:56, 0:64], both[0:56, 64:128]], axis=0)
    total = both[56:57, 0:1]
    p_ref[...] = p
    top = jnp.max(jnp.abs(p), axis=0, keepdims=True)
    weight = steps_ref[0].astype(F32) / total
    unit = p * (1.0 / jnp.maximum(top, 1e-37)) * weight
    flat = unit.T
    upper = flat.astype(BF).astype(F32)
    rest = flat - upper
    lhs_ref[0:64, :] = jnp.concatenate([upper, upper], axis=1).astype(BF)
    lhs_ref[64:128, :] = jnp.concatenate([rest, rest], axis=1).astype(BF)
    gram_ref[...] = jnp.zeros_like(gram_ref)
    gram_ref[0:64, 0:64] = lax.dot_general(p, p, (((0,), (0,)), ((), ())), precision=lax.Precision.HIGHEST, preferred_element_type=F32)
    gram_ref[64:65, 0:64] = top


def prepare(steps, a, b, c, d):
    return pl.pallas_call(
        prep_kernel,
        in_specs=[SM, VM, VM, VM, VM],
        out_specs=[VM, VM, VM],
        out_shape=[
            jax.ShapeDtypeStruct((112, 64), F32),
            jax.ShapeDtypeStruct((128, 224), BF),
            jax.ShapeDtypeStruct((72, 128), F32),
        ],
        compiler_params=params_of(),
        name="prepare",
    )(steps, a, b, c, d)


def blocks_of(tiles):
    return [(i, i + tiles) for i in range(0, HALF, tiles)]


def columns(side, begin, end):
    return pl.ds(pl.multiple_of(side * (HALF * 128) + begin * 128, 128), (end - begin) * 128)


def load_block(side, s, begin, end, d_ref, e_ref, both_ref, sem):
    src = columns(side, begin, end)
    return [
        start(d_ref.at[0, :, src], both_ref.at[s, 0:112, :], sem.at[s, 0]),
        start(e_ref.at[0, :, src], both_ref.at[s, 112:224, :], sem.at[s, 1]),
    ]


def chunk_range(k):
    return slice(FIRST[k], FIRST[k] + COUNTS[k])


def q_half(where, lhs, delta, error, far):
    parts = blocks_of(28)
    n = len(parts)

    def kernel(s_ref, lhs_ref, d_ref, e_ref, *rest):
        out_refs, (both_ref, v_ref, sem, out_sem) = rest[:3], rest[3:]
        side = 1 - s_ref[0] if far else s_ref[0]
        copies = [load_block(side, s, *parts[s], d_ref, e_ref, both_ref, sem) for s in range(n)]
        outs = []
        for s, (begin, end) in enumerate(parts):
            for copy in copies[s]:
                copy.wait()
            r = lax.dot_general(lhs_ref[...], both_ref[s], (((1,), (0,)), ((), ())), preferred_element_type=F32)
            v = r[0:64] + r[64:128]
            for i in range(8):
                for t in range(end - begin):
                    v_ref[i, begin + t] = v[8 * i:8 * i + 8, 128 * t:128 * t + 128]
            while len(outs) < 3 and FIRST[len(outs)] + COUNTS[len(outs)] <= end:
                k = len(outs)
                outs.append(start(v_ref.at[:, chunk_range(k)], out_refs[k], out_sem.at[k]))
        for copy in outs:
            copy.wait()

    return pl.pallas_call(
        kernel,
        in_specs=[SM, VM, HBM, HBM],
        out_specs=[ANY] * 3,
        out_shape=[jax.ShapeDtypeStruct((8, c, 8, 128), F32) for c in COUNTS],
        scratch_shapes=[
            pltpu.VMEM((n, 224, 28 * 128), BF),
            pltpu.VMEM((8, HALF, 8, 128), F32),
            DMA((n, 2)),
            DMA((3,)),
        ],
        compiler_params=params_of(),
        cost_estimate=pl.CostEstimate(flops=2 * 128 * 224 * HALF * 128, bytes_accessed=HALF * 128 * (448 + 256), transcendentals=0),
        name="q_far" if far else "q_own",
    )(where, lhs, delta, error)


def scales_kernel(own_ref, near_ref, pair_ref, far_ref, both_ref, f_own_ref, f_near_ref):
    join = jnp.where(lax.broadcasted_iota(jnp.int32, (72, 128), 0) == 64, jnp.maximum(pair_ref[...], far_ref[...]), pair_ref[...] + far_ref[...])
    both_ref[...] = join
    eye = lax.broadcasted_iota(jnp.int32, (64, 64), 0) == lax.broadcasted_iota(jnp.int32, (64, 64), 1)
    top = jnp.maximum(join[64:65, 0:64], 1e-37)
    for src, dst in ((own_ref, f_own_ref), (near_ref, f_near_ref)):
        ratio = src[64:65, 0:64] / top
        column = jnp.sum(jnp.where(eye, ratio, 0.0), axis=1, keepdims=True)
        dst[...] = jnp.broadcast_to(column, (64, 128))


def scales(own, near, pair, far):
    return pl.pallas_call(
        scales_kernel,
        in_specs=[VM] * 4,
        out_specs=[VM] * 3,
        out_shape=[jax.ShapeDtypeStruct((72, 128), F32)] + [jax.ShapeDtypeStruct((64, 128), F32)] * 2,
        compiler_params=params_of(8),
        name="scales",
    )(own, near, pair, far)


def solve_kernel(gram_ref, p_ref, pass_in, w_ref, pass_out):
    highest = lax.Precision.HIGHEST
    row = lax.broadcasted_iota(jnp.int32, (64, 64), 0)
    lane = lax.broadcasted_iota(jnp.int32, (64, 64), 1)
    eye = (row == lane).astype(F32)
    inv_row = 1.0 / jnp.maximum(gram_ref[64:65, 0:64], 1e-37)
    inv_col = jnp.sum(eye * inv_row, axis=1, keepdims=True)
    unit = gram_ref[0:64, 0:64] * inv_col * inv_row
    m = jnp.concatenate([unit, eye], axis=1)
    below = lax.broadcasted_iota(jnp.int32, (64, 1), 0)
    for k in range(64):
        factor = jnp.where(below > k, m[:, k:k + 1], 0.0)
        m = m - factor * (m[k:k + 1, :] * (1.0 / m[k:k + 1, k:k + 1]))
    pivots = jnp.sum(eye * m[:, 0:64], axis=1, keepdims=True)
    inverse = m[:, 64:128] * (1.0 / jnp.sqrt(pivots))
    p_hat = lax.dot_general(p_ref[...] * inv_row, inverse, (((1,), (1,)), ((), ())), precision=highest, preferred_element_type=F32)
    w = lax.dot_general(p_hat, inverse, (((1,), (0,)), ((), ())), precision=highest, preferred_element_type=F32)
    upper = w.astype(BF).astype(F32)
    w_ref[...] = jnp.concatenate([upper, upper, w - upper], axis=1).astype(BF)


def solve(gram, p, through):
    return pl.pallas_call(
        solve_kernel,
        in_specs=[VM, VM, ANY],
        out_specs=[VM, ANY],
        out_shape=[jax.ShapeDtypeStruct((112, 192), BF), jax.ShapeDtypeStruct(through.shape, F32)],
        input_output_aliases={2: 1},
        compiler_params=params_of(8),
        cost_estimate=pl.CostEstimate(flops=10 ** 7, bytes_accessed=10 ** 7, transcendentals=0),
        name="solve",
    )(gram, p, through)


def finish(where, w, sides, delta, error, params, momentum, base, far):
    parts = blocks_of(14)
    n = len(parts)
    wide = 14 * 128
    given = len(base)

    def kernel(s_ref, w_ref, *rest):
        q_refs, (d_ref, e_ref, par_ref, mom_ref), rest = rest[:6], rest[6:10], rest[10 + given:]
        err_ref, np_ref, nm_ref, both_ref, q_ref, new_ref, pb_ref, mb_ref, po_ref, mo_ref, sem, q_sem, out_sem, par_sem = rest
        side = 1 - s_ref[0] if far else s_ref[0]
        turn_of = s_ref[4] - 8 * side
        mine = (turn_of >= 0) & (turn_of < 8)

        q_copies, copies = [], []
        for s in range(n):
            copies.append(load_block(side, s, *parts[s], d_ref, e_ref, both_ref, sem))
            k = len(q_copies)
            if k < 3 and s % 2 == 0:
                bit = s_ref[1 + k]
                q_copies.append([
                    start(q_refs[2 * k], q_ref.at[pl.ds(bit * 4, 4), chunk_range(k)], q_sem.at[k, 0]),
                    start(q_refs[2 * k + 1], q_ref.at[pl.ds((1 - bit) * 4, 4), chunk_range(k)], q_sem.at[k, 1]),
                ])

        @pl.when(mine)
        def _():
            start(par_ref, pb_ref, par_sem.at[0])
            start(mom_ref, mb_ref, par_sem.at[1])

        outs = []
        for s, (begin, end) in enumerate(parts):
            while q_copies and FIRST[3 - len(q_copies)] < end:
                for copy in q_copies.pop(0):
                    copy.wait()
            for copy in copies[s]:
                copy.wait()
            q = jnp.concatenate([jnp.concatenate([q_ref[i, t] for t in range(begin, end)], axis=1) for i in range(8)], axis=0)
            upper = q.astype(BF)
            below = (q - upper.astype(F32)).astype(BF)
            rhs = jnp.concatenate([upper, below, upper], axis=0)
            approx = lax.dot_general(w_ref[...], rhs, (((1,), (0,)), ((), ())), preferred_element_type=F32)
            merged = both_ref[s, 0:112, :].astype(F32) + both_ref[s, 112:224, :].astype(F32)
            new_ref[s] = (merged - approx).astype(BF)
            outs.append(start(new_ref.at[s], err_ref.at[0, :, columns(side, begin, end)], out_sem.at[s]))

            @pl.when(turn_of == s)
            def _():
                pltpu.make_async_copy(par_ref, pb_ref, par_sem.at[0]).wait()
                pltpu.make_async_copy(mom_ref, mb_ref, par_sem.at[1]).wait()
                fresh = beta * mb_ref[...] + approx
                mo_ref[...] = fresh
                po_ref[...] = pb_ref[...] - outer_lr * (approx + beta * fresh)
                start(po_ref, np_ref, par_sem.at[2])
                start(mo_ref, nm_ref, par_sem.at[3])

        for copy in outs:
            copy.wait()

        @pl.when(mine)
        def _():
            pltpu.make_async_copy(po_ref, np_ref, par_sem.at[2]).wait()
            pltpu.make_async_copy(mo_ref, nm_ref, par_sem.at[3]).wait()

    panel = pltpu.VMEM((112, wide), F32)
    return pl.pallas_call(
        kernel,
        in_specs=[SM, VM] + [ANY] * 6 + [HBM] * (4 + given),
        out_specs=[HBM, HBM, HBM],
        out_shape=[
            jax.ShapeDtypeStruct(delta.shape, BF),
            jax.ShapeDtypeStruct(params.shape, F32),
            jax.ShapeDtypeStruct(params.shape, F32),
        ],
        input_output_aliases={12 + i: i for i in range(given)},
        scratch_shapes=[
            pltpu.VMEM((n, 224, wide), BF),
            pltpu.VMEM((8, HALF, 8, 128), F32),
            pltpu.VMEM((n, 112, wide), BF),
            panel, panel, panel, panel,
            DMA((n, 2)),
            DMA((3, 2)),
            DMA((n,)),
            DMA((4,)),
        ],
        compiler_params=params_of(),
        cost_estimate=pl.CostEstimate(flops=2 * 112 * 192 * HALF * 128, bytes_accessed=HALF * 128 * (672 + 256), transcendentals=0),
        name="finish_far" if far else "finish_own",
    )(where, w, *sides, delta, error, params, momentum, *base)


def local(delta, error, steps, q_start, params, momentum):
    place = {a: lax.axis_index(a) for a in AXES}
    core = place["c"]
    hi_bit = {a: place[a] // 2 for a in REP + ("y",)}
    lo_bit = {a: (place[a] + place[a] // 2) % 2 for a in REP + ("y",)}
    where = jnp.stack([core] + [lo_bit[r[0]] for r in ROUTES] + [lax.axis_index(REP)])

    own = left_factor(delta, error, q_start.T, steps)
    own = (own + turn(own, "x", 2)) + (turn(own, "x", 1) + turn(own, "x", 3))
    p_all, lhs, gram_own = prepare(steps, own, turn(own, "z", 2), turn(own, "z", 1), turn(own, "z", 3))

    row64 = lax.broadcasted_iota(jnp.int32, gram_own.shape, 0) == 64
    join = lambda a, b: jnp.where(row64, jnp.maximum(a, b), a + b)
    gram_near = swap(gram_own)
    chip = join(gram_own, gram_near)
    pair = join(chip, low(chip, "y"))
    both, f_own, f_near = scales(gram_own, gram_near, pair, high(pair, "y"))
    f_own, f_near = f_own.reshape(8, 1, 8, 128), f_near.reshape(8, 1, 8, 128)

    arrived = [swap(v) for v in q_half(where, lhs, delta, error, True)]
    terms = q_half(where, lhs, delta, error, False)
    half = lambda x, b: lax.dynamic_slice_in_dim(x, b * (x.shape[0] // 2), x.shape[0] // 2, 0)
    parts = []
    for k, route in enumerate(ROUTES):
        blend = lambda b: half(terms[k], b) * half(f_own, b) + half(arrived[k], b) * half(f_near, b)
        bit = lo_bit[route[0]]
        send, keep = blend(1 - bit), blend(bit)
        got = low(send, route[0])
        if k == 2:
            w_cat, keep = solve(both, p_all, keep)
        for d in route[1:]:
            take = lambda b: half(keep, b) + half(got, b)
            send, keep = take(1 - lo_bit[d]), take(lo_bit[d])
            got = low(send, d)
        parts.append(keep[0] + got[0])
    mine = jnp.concatenate(parts, axis=0)
    mine = half(mine, hi_bit["y"]) + high(half(mine, 1 - hi_bit["y"]), "y")
    quarter = lambda a, b: lax.dynamic_slice_in_dim(mine, (2 * a + b) * 14, 14, 0)
    hz, hx = hi_bit["z"], hi_bit["x"]
    both_high = lambda x: lax.ppermute(x, REP, [(4 * i + j, 4 * (3 - i) + 3 - j) for i in range(4) for j in range(4)])
    mine = (quarter(hz, hx) + both_high(quarter(1 - hz, 1 - hx))) + (high(quarter(1 - hz, hx), "z") + high(quarter(hz, 1 - hx), "x"))

    def in_order(bit, a, b):
        return jnp.where(bit == 0, jnp.concatenate([a, b], 0), jnp.concatenate([b, a], 0))

    across = {0: mine, 1: high(mine, "x"), 2: high(mine, "z"), 3: both_high(mine)}
    by_x = [in_order(hx, across[m], across[m + 1]) for m in (0, 2)]
    mine = in_order(hz, *by_x)
    mine = in_order(hi_bit["y"], mine, high(mine, "y"))
    sides = []
    for k, route in enumerate(ROUTES):
        v = mine[chunk_range(k)][None]
        for d in route[:0:-1]:
            v = in_order(lo_bit[d], v, low(v, d))
        sides.append((v, low(v, route[0])))
    far = [swap(x) for pair in sides for x in pair]
    near = [x for pair in sides for x in pair]
    base = finish(where, w_cat, near, delta, error, params, momentum, (), False)
    base = finish(where, w_cat, far, delta, error, params, momentum, base, True)
    error_new, params_new, momentum_new = base
    return (params_new, momentum_new, error_new)


def solution(mesh):
    fine = Mesh(mesh.devices.reshape(4, 4, 4, 2), AXES)
    in_specs = (
        P(REP, ROW, None),
        P(REP, ROW, None),
        P(REP),
        P(),
        P(ROW, REP),
        P(ROW, REP),
    )
    out_specs = (P(ROW, REP), P(ROW, REP), P(REP, ROW, None))
    return jax.shard_map(local, mesh=fine, in_specs=in_specs, out_specs=out_specs, check_vma=False)
```

```python
import jax
import jax.numpy as jnp
from jax import lax
from jax.experimental import pallas as pl
from jax.experimental.pallas import tpu as pltpu
from jax.sharding import Mesh, PartitionSpec as P

outer_lr = 0.7
beta = 0.9

AXES = ("z", "x", "y", "c")
REP = ("z", "x")
ROW = ("y", "c")
ROUTES = (("x", "y", "z"), ("y", "z", "x"), ("z", "x", "y"))

HALF = 112
COUNTS = (37, 37, 38)
FIRST = (0, 37, 74)
BF = jnp.bfloat16
F32 = jnp.float32
HBM = pl.BlockSpec(memory_space=pltpu.HBM)
ANY = pl.BlockSpec(memory_space=pl.ANY)
VM = pl.BlockSpec(memory_space=pltpu.VMEM)
SM = pl.BlockSpec(memory_space=pltpu.SMEM)
DMA = pltpu.SemaphoreType.DMA


def params_of(mib=58):
    return pltpu.CompilerParams(vmem_limit_bytes=mib << 20)


def turn(x, axis, step):
    return lax.ppermute(x, axis, [(i, (i + step) % 4) for i in range(4)])


def low(x, axis):
    return lax.ppermute(x, axis, [(i, i ^ 1) for i in range(4)])


def high(x, axis):
    return lax.ppermute(x, axis, [(i, 3 - i) for i in range(4)])


def swap(x):
    return lax.ppermute(x, "c", [(0, 1), (1, 0)])


def start(src, dst, sem):
    copy = pltpu.make_async_copy(src, dst, sem)
    copy.start()
    return copy


P_BLOCK = 4096


def p_kernel(steps_ref, d_ref, e_ref, q_ref, out_ref, both_ref, qb_ref, sem):
    n = d_ref.shape[2] // P_BLOCK
    copies = []
    for i in range(n):
        cols = slice(i * P_BLOCK, (i + 1) * P_BLOCK)
        copies.append((
            start(d_ref.at[0, :, cols], both_ref.at[0:112, cols], sem.at[i, 0]),
            start(e_ref.at[0, :, cols], both_ref.at[112:224, cols], sem.at[i, 1]),
            start(q_ref.at[:, cols], qb_ref.at[:, cols], sem.at[i, 2]),
        ))
    acc_d = jnp.zeros((112, 64), F32)
    acc_e = jnp.zeros((112, 64), F32)
    dims = (((1,), (1,)), ((), ()))
    for i in range(n):
        cols = slice(i * P_BLOCK, (i + 1) * P_BLOCK)
        for copy in copies[i]:
            copy.wait()
        acc_d = acc_d + lax.dot_general(both_ref[0:112, cols], qb_ref[:, cols], dims, preferred_element_type=F32)
        acc_e = acc_e + lax.dot_general(both_ref[112:224, cols], qb_ref[:, cols], dims, preferred_element_type=F32)
    count = steps_ref[0].astype(F32)
    p = count * (acc_d + acc_e)
    out_ref[56:64, :] = jnp.full((8, 128), count, F32)
    out_ref[0:56, :] = jnp.concatenate([p[0:56], p[56:112]], axis=1)


def left_factor(delta, error, q_t, steps):
    width = delta.shape[2]
    return pl.pallas_call(
        p_kernel,
        in_specs=[SM, HBM, HBM, HBM],
        out_specs=VM,
        out_shape=jax.ShapeDtypeStruct((64, 128), F32),
        scratch_shapes=[
            pltpu.VMEM((224, width), BF),
            pltpu.VMEM((64, width), BF),
            DMA((width // P_BLOCK, 3)),
        ],
        compiler_params=params_of(),
        name="left_factor",
    )(steps, delta, error, q_t)


def prep_kernel(steps_ref, a_ref, b_ref, c_ref, d_ref, p_ref, lhs_ref, gram_ref):
    both = (a_ref[...] + b_ref[...]) + (c_ref[...] + d_ref[...])
    p = jnp.concatenate([both[0:56, 0:64], both[0:56, 64:128]], axis=0)
    total = both[56:57, 0:1]
    p_ref[...] = p
    top = jnp.max(jnp.abs(p), axis=0, keepdims=True)
    weight = steps_ref[0].astype(F32) / total
    unit = p * (1.0 / jnp.maximum(top, 1e-37)) * weight
    flat = unit.T
    upper = flat.astype(BF).astype(F32)
    rest = flat - upper
    lhs_ref[0:64, :] = jnp.concatenate([upper, upper], axis=1).astype(BF)
    lhs_ref[64:128, :] = jnp.concatenate([rest, rest], axis=1).astype(BF)
    gram_ref[...] = jnp.zeros_like(gram_ref)
    gram_ref[0:64, 0:64] = lax.dot_general(p, p, (((0,), (0,)), ((), ())), precision=lax.Precision.HIGHEST, preferred_element_type=F32)
    gram_ref[64:65, 0:64] = top


def prepare(steps, a, b, c, d):
    return pl.pallas_call(
        prep_kernel,
        in_specs=[SM, VM, VM, VM, VM],
        out_specs=[VM, VM, VM],
        out_shape=[
            jax.ShapeDtypeStruct((112, 64), F32),
            jax.ShapeDtypeStruct((128, 224), BF),
            jax.ShapeDtypeStruct((72, 128), F32),
        ],
        compiler_params=params_of(8),
        name="prepare",
    )(steps, a, b, c, d)


def blocks_of(tiles):
    return [(i, i + tiles) for i in range(0, HALF, tiles)]


def columns(side, begin, end):
    return pl.ds(pl.multiple_of(side * (HALF * 128) + begin * 128, 128), (end - begin) * 128)


def load_block(side, s, begin, end, d_ref, e_ref, both_ref, sem):
    src = columns(side, begin, end)
    return [
        start(d_ref.at[0, :, src], both_ref.at[s, 0:112, :], sem.at[s, 0]),
        start(e_ref.at[0, :, src], both_ref.at[s, 112:224, :], sem.at[s, 1]),
    ]


def chunk_range(k):
    return slice(FIRST[k], FIRST[k] + COUNTS[k])


def q_half(where, lhs, delta, error, far, *first):
    parts = blocks_of(28)
    n = len(parts)

    def kernel(s_ref, lhs_ref, d_ref, e_ref, *rest):
        rest = rest[len(first):]
        out_refs, (both_ref, v_ref, sem, out_sem) = rest[:3], rest[3:]
        side = 1 - s_ref[0] if far else s_ref[0]
        copies = [load_block(side, s, *parts[s], d_ref, e_ref, both_ref, sem) for s in range(n)]
        outs = []
        for s, (begin, end) in enumerate(parts):
            for copy in copies[s]:
                copy.wait()
            r = lax.dot_general(lhs_ref[...], both_ref[s], (((1,), (0,)), ((), ())), preferred_element_type=F32)
            v = r[0:64] + r[64:128]
            for i in range(8):
                for t in range(end - begin):
                    v_ref[i, begin + t] = v[8 * i:8 * i + 8, 128 * t:128 * t + 128]
            while len(outs) < 3 and FIRST[len(outs)] + COUNTS[len(outs)] <= end:
                k = len(outs)
                outs.append(start(v_ref.at[:, chunk_range(k)], out_refs[k], out_sem.at[k]))
        for copy in outs:
            copy.wait()

    return pl.pallas_call(
        kernel,
        in_specs=[SM, VM, HBM, HBM] + [ANY] * len(first),
        out_specs=[HBM] * 3,
        out_shape=[jax.ShapeDtypeStruct((8, c, 8, 128), F32) for c in COUNTS],
        scratch_shapes=[
            pltpu.VMEM((n, 224, 28 * 128), BF),
            pltpu.VMEM((8, HALF, 8, 128), F32),
            DMA((n, 2)),
            DMA((3,)),
        ],
        compiler_params=params_of(),
        cost_estimate=pl.CostEstimate(flops=2 * 128 * 224 * HALF * 128, bytes_accessed=HALF * 128 * (448 + 256), transcendentals=0),
        name="q_far" if far else "q_own",
    )(where, lhs, delta, error, *first)


def blend(where, terms, arrived, f_own, f_near, gram):
    def kernel(s_ref, *refs):
        a_refs, b_refs, (f_ref, g_ref, gram_ref), refs = refs[:3], refs[3:6], refs[6:9], refs[9:]
        keep_refs, send_refs, (a_buf, b_buf, sem, out_sem) = refs[:3], refs[3:6], refs[6:]
        copies = []
        for k in range(3):
            copies.append((
                start(a_refs[k], a_buf.at[:, chunk_range(k)], sem.at[k, 0]),
                start(b_refs[k], b_buf.at[:, chunk_range(k)], sem.at[k, 1]),
            ))
        outs = []
        for k in range(3):
            for copy in copies[k]:
                copy.wait()
            tiles = chunk_range(k)
            for i in range(8):
                f = f_ref[8 * i:8 * i + 8, :][None]
                g = g_ref[8 * i:8 * i + 8, :][None]
                a_buf[i, tiles] = f * a_buf[i, tiles] + g * b_buf[i, tiles]
            bit = s_ref[1 + k]
            outs.append(start(a_buf.at[pl.ds(bit * 4, 4), tiles], keep_refs[k], out_sem.at[k, 4]))
            for i in range(4):
                place = slice(i * COUNTS[k], (i + 1) * COUNTS[k])
                outs.append(start(a_buf.at[(1 - bit) * 4 + i, tiles], send_refs[k].at[place], out_sem.at[k, i]))
            if ROUTES[k][0] == "y":
                outs.append(start(gram_ref, send_refs[k].at[slice(4 * COUNTS[k], 4 * COUNTS[k] + 9)], out_sem.at[k, 5]))
        for copy in outs:
            copy.wait()

    halves = [jax.ShapeDtypeStruct((4, c, 8, 128), F32) for c in COUNTS]
    away = [jax.ShapeDtypeStruct((4 * c + (9 if r[0] == "y" else 0), 8, 128), F32) for c, r in zip(COUNTS, ROUTES)]
    out = pl.pallas_call(
        kernel,
        in_specs=[SM] + [ANY] * 6 + [VM, VM, VM],
        out_specs=[HBM] * 6,
        out_shape=halves + away,
        scratch_shapes=[
            pltpu.VMEM((8, HALF, 8, 128), F32),
            pltpu.VMEM((8, HALF, 8, 128), F32),
            DMA((3, 2)),
            DMA((3, 6)),
        ],
        compiler_params=params_of(16),
        cost_estimate=pl.CostEstimate(flops=10 ** 6, bytes_accessed=11 * 10 ** 6, transcendentals=0),
        name="blend",
    )(where, *terms, *arrived, f_own, f_near, gram.reshape(9, 8, 128))
    return out[:3], out[3:]


def scales_kernel(a_ref, b_ref, *refs):
    sum_ref, f_a_ref, f_b_ref = refs[-3:]
    both = [ref[...] for ref in refs[:-3]]
    maxima = lax.broadcasted_iota(jnp.int32, (72, 128), 0) == 64
    while len(both) > 1:
        n = len(both) // 2
        both = [jnp.where(maxima, jnp.maximum(c, d), c + d) for c, d in zip(both[:n], both[n:])]
    both = both[0]
    sum_ref[...] = both
    eye = lax.broadcasted_iota(jnp.int32, (64, 64), 0) == lax.broadcasted_iota(jnp.int32, (64, 64), 1)
    top = jnp.maximum(both[64:65, 0:64], 1e-37)
    for src, dst in ((a_ref, f_a_ref), (b_ref, f_b_ref)):
        column = jnp.sum(jnp.where(eye, src[64:65, 0:64] / top, 0.0), axis=1, keepdims=True)
        dst[...] = jnp.broadcast_to(column, (64, 128))


def scales(a, b, *terms):
    both, f_a, f_b = pl.pallas_call(
        scales_kernel,
        in_specs=[VM] * (2 + len(terms)),
        out_specs=[VM] * 3,
        out_shape=[jax.ShapeDtypeStruct((72, 128), F32)] + [jax.ShapeDtypeStruct((64, 128), F32)] * 2,
        compiler_params=params_of(8),
        name="scales",
    )(a, b, *terms)
    return both, f_a, f_b


def solve_kernel(gram_ref, p_ref, block_ref, w_ref, block_out, sem):
    copy = start(block_ref, block_out, sem)
    highest = lax.Precision.HIGHEST
    row = lax.broadcasted_iota(jnp.int32, (64, 64), 0)
    lane = lax.broadcasted_iota(jnp.int32, (64, 64), 1)
    eye = (row == lane).astype(F32)
    inv_row = 1.0 / jnp.maximum(gram_ref[64:65, 0:64], 1e-37)
    inv_col = jnp.sum(eye * inv_row, axis=1, keepdims=True)
    unit = gram_ref[0:64, 0:64] * inv_col * inv_row
    m = jnp.concatenate([unit, eye], axis=1)
    below = lax.broadcasted_iota(jnp.int32, (64, 1), 0)
    for k in range(64):
        factor = jnp.where(below > k, m[:, k:k + 1], 0.0)
        m = m - factor * (m[k:k + 1, :] * (1.0 / m[k:k + 1, k:k + 1]))
    pivots = jnp.sum(eye * m[:, 0:64], axis=1, keepdims=True)
    inverse = m[:, 64:128] * (1.0 / jnp.sqrt(pivots))
    p_hat = lax.dot_general(p_ref[...] * inv_row, inverse, (((1,), (1,)), ((), ())), precision=highest, preferred_element_type=F32)
    w = lax.dot_general(p_hat, inverse, (((1,), (0,)), ((), ())), precision=highest, preferred_element_type=F32)
    upper = w.astype(BF).astype(F32)
    w_ref[...] = jnp.concatenate([upper, upper, w - upper], axis=1).astype(BF)
    copy.wait()


def solve(gram, p, block):
    return pl.pallas_call(
        solve_kernel,
        in_specs=[VM, VM, ANY],
        out_specs=[VM, HBM],
        out_shape=[jax.ShapeDtypeStruct((112, 192), BF), jax.ShapeDtypeStruct(block.shape, F32)],
        scratch_shapes=[DMA(())],
        compiler_params=params_of(8),
        cost_estimate=pl.CostEstimate(flops=10 ** 7, bytes_accessed=10 ** 7, transcendentals=0),
        name="solve",
    )(gram, p, block)


def finish(where, w, sides, delta, error, params, momentum, base, far):
    parts = blocks_of(14)
    n = len(parts)
    wide = 14 * 128
    given = len(base)

    def kernel(s_ref, w_ref, *rest):
        q_refs, (d_ref, e_ref, par_ref, mom_ref), rest = rest[:6], rest[6:10], rest[10 + given:]
        err_ref, np_ref, nm_ref, both_ref, q_ref, new_ref, pb_ref, mb_ref, po_ref, mo_ref, sem, q_sem, out_sem, par_sem = rest
        side = 1 - s_ref[0] if far else s_ref[0]
        turn_of = s_ref[4] - 8 * side
        mine = (turn_of >= 0) & (turn_of < 8)

        q_copies, copies = [], []
        for s in range(n):
            copies.append(load_block(side, s, *parts[s], d_ref, e_ref, both_ref, sem))
            k = len(q_copies)
            if k < 3 and s % 2 == 0:
                bit = s_ref[1 + k]
                q_copies.append([
                    start(q_refs[2 * k], q_ref.at[pl.ds(bit * 4, 4), chunk_range(k)], q_sem.at[k, 0]),
                    start(q_refs[2 * k + 1], q_ref.at[pl.ds((1 - bit) * 4, 4), chunk_range(k)], q_sem.at[k, 1]),
                ])

        @pl.when(mine)
        def _():
            start(par_ref, pb_ref, par_sem.at[0])
            start(mom_ref, mb_ref, par_sem.at[1])

        outs = []
        for s, (begin, end) in enumerate(parts):
            while q_copies and FIRST[3 - len(q_copies)] < end:
                for copy in q_copies.pop(0):
                    copy.wait()
            for copy in copies[s]:
                copy.wait()
            q = jnp.concatenate([jnp.concatenate([q_ref[i, t] for t in range(begin, end)], axis=1) for i in range(8)], axis=0)
            upper = q.astype(BF)
            below = (q - upper.astype(F32)).astype(BF)
            rhs = jnp.concatenate([upper, below, upper], axis=0)
            approx = lax.dot_general(w_ref[...], rhs, (((1,), (0,)), ((), ())), preferred_element_type=F32)
            merged = both_ref[s, 0:112, :].astype(F32) + both_ref[s, 112:224, :].astype(F32)
            new_ref[s] = (merged - approx).astype(BF)
            outs.append(start(new_ref.at[s], err_ref.at[0, :, columns(side, begin, end)], out_sem.at[s]))

            @pl.when(turn_of == s)
            def _():
                pltpu.make_async_copy(par_ref, pb_ref, par_sem.at[0]).wait()
                pltpu.make_async_copy(mom_ref, mb_ref, par_sem.at[1]).wait()
                fresh = beta * mb_ref[...] + approx
                mo_ref[...] = fresh
                po_ref[...] = pb_ref[...] - outer_lr * (approx + beta * fresh)
                start(po_ref, np_ref, par_sem.at[2])
                start(mo_ref, nm_ref, par_sem.at[3])

        for copy in outs:
            copy.wait()

        @pl.when(mine)
        def _():
            pltpu.make_async_copy(po_ref, np_ref, par_sem.at[2]).wait()
            pltpu.make_async_copy(mo_ref, nm_ref, par_sem.at[3]).wait()

    panel = pltpu.VMEM((112, wide), F32)
    return pl.pallas_call(
        kernel,
        in_specs=[SM, VM] + [ANY] * 6 + [HBM] * (4 + given),
        out_specs=[HBM, HBM, HBM],
        out_shape=[
            jax.ShapeDtypeStruct(delta.shape, BF),
            jax.ShapeDtypeStruct(params.shape, F32),
            jax.ShapeDtypeStruct(params.shape, F32),
        ],
        input_output_aliases={12 + i: i for i in range(given)},
        scratch_shapes=[
            pltpu.VMEM((n, 224, wide), BF),
            pltpu.VMEM((8, HALF, 8, 128), F32),
            pltpu.VMEM((n, 112, wide), BF),
            panel, panel, panel, panel,
            DMA((n, 2)),
            DMA((3, 2)),
            DMA((n,)),
            DMA((4,)),
        ],
        compiler_params=params_of(),
        cost_estimate=pl.CostEstimate(flops=2 * 112 * 192 * HALF * 128, bytes_accessed=HALF * 128 * (672 + 256), transcendentals=0),
        name="finish_far" if far else "finish_own",
    )(where, w, *sides, delta, error, params, momentum, *base)


def local(delta, error, steps, q_start, params, momentum):
    place = {a: lax.axis_index(a) for a in AXES}
    core = place["c"]
    hi_bit = {a: place[a] // 2 for a in REP + ("y",)}
    lo_bit = {a: (place[a] + place[a] // 2) % 2 for a in REP + ("y",)}
    where = jnp.stack([core] + [lo_bit[r[0]] for r in ROUTES] + [lax.axis_index(REP)])

    own = left_factor(delta, error, q_start.T, steps)
    own = (own + turn(own, "x", 2)) + (turn(own, "x", 1) + turn(own, "x", 3))
    p_all, lhs, gram_own = prepare(steps, own, turn(own, "z", 2), turn(own, "z", 1), turn(own, "z", 3))

    gram_near = swap(gram_own)
    chip, f_own, f_near = scales(gram_own, gram_near, gram_own, gram_near)

    arrived = [swap(v) for v in q_half(where, lhs, delta, error, True)]
    terms = q_half(where, lhs, delta, error, False)
    keeps, sends = blend(where, terms, arrived, f_own, f_near, chip)
    half = lambda x, b: lax.dynamic_slice_in_dim(x, b * (x.shape[0] // 2), x.shape[0] // 2, 0)
    gots = [low(send, route[0]) for send, route in zip(sends, ROUTES)]
    rest = 4 * COUNTS[1]
    chip_near = gots[1][rest:].reshape(72, 128)
    gots = [got[:4 * c].reshape(4, c, 8, 128) for got, c in zip(gots, COUNTS)]
    pair, g_own, g_near = scales(chip, chip_near, chip, chip_near)
    parts = []
    for k, route in enumerate(ROUTES):
        keep, got = keeps[k], gots[k]
        ours, theirs = [g.reshape(8, 1, 8, 128) for g in (g_own, g_near)]
        for step in range(3):
            ours, theirs = [half(g, lo_bit[route[step]]) for g in (ours, theirs)]
            scaled = route[step] == "y"
            if step == 2:
                parts.append(keep[0] * ours[0] + got[0] * theirs[0] if scaled else keep[0] + got[0])
                break
            bit = lo_bit[route[step + 1]]

            def take(b):
                if scaled:
                    return half(keep, b) * half(ours, b) + half(got, b) * half(theirs, b)
                return half(keep, b) + half(got, b)

            send, keep = take(1 - bit), take(bit)
            got = low(send, route[step + 1])
    mine = jnp.concatenate(parts, axis=0)
    got = high(jnp.concatenate([half(mine, 1 - hi_bit["y"]), pair.reshape(9, 8, 128)], axis=0), "y")
    pair_near = got[56:].reshape(72, 128)
    both, h_own, h_near = scales(pair, pair_near, pair, pair_near)

    def per_tile(h):
        rows = h.reshape(8, 8, 128)
        spread = []
        for k, route in enumerate(ROUTES):
            block = sum(lo_bit[d] * (4 >> i) for i, d in enumerate(route))
            spread.append(jnp.broadcast_to(lax.dynamic_slice_in_dim(rows, block, 1, 0), (COUNTS[k], 8, 128)))
        return half(jnp.concatenate(spread, axis=0), hi_bit["y"])

    mine = half(mine, hi_bit["y"]) * per_tile(h_own) + got[:56] * per_tile(h_near)
    quarter = lambda a, b: lax.dynamic_slice_in_dim(mine, (2 * a + b) * 14, 14, 0)
    hz, hx = hi_bit["z"], hi_bit["x"]
    both_high = lambda x: lax.ppermute(x, REP, [(4 * i + j, 4 * (3 - i) + 3 - j) for i in range(4) for j in range(4)])
    mine = (quarter(hz, hx) + both_high(quarter(1 - hz, 1 - hx))) + (high(quarter(1 - hz, hx), "z") + high(quarter(hz, 1 - hx), "x"))

    def in_order(bit, a, b):
        return jnp.where(bit == 0, jnp.concatenate([a, b], 0), jnp.concatenate([b, a], 0))

    across = {0: mine, 1: high(mine, "x"), 2: high(mine, "z"), 3: both_high(mine)}
    by_x = [in_order(hx, across[m], across[m + 1]) for m in (0, 2)]
    mine = in_order(hz, *by_x)
    mine = in_order(hi_bit["y"], mine, high(mine, "y"))
    sides = []
    for k, route in enumerate(ROUTES):
        v = mine[chunk_range(k)][None]
        for d in route[:0:-1]:
            v = in_order(lo_bit[d], v, low(v, d))
        sides.append((v, low(v, route[0])))
    w_cat, last = solve(both, p_all, sides[2][0])
    far = [swap(x) for pair in sides[:2] for x in pair] + [swap(last), swap(sides[2][1])]
    near = [x for pair in sides for x in pair]
    base = finish(where, w_cat, near, delta, error, params, momentum, (), False)
    base = finish(where, w_cat, far, delta, error, params, momentum, base, True)
    error_new, params_new, momentum_new = base
    return (params_new, momentum_new, error_new)


def solution(mesh):
    fine = Mesh(mesh.devices.reshape(4, 4, 4, 2), AXES)
    in_specs = (
        P(REP, ROW, None),
        P(REP, ROW, None),
        P(REP),
        P(),
        P(ROW, REP),
        P(ROW, REP),
    )
    out_specs = (P(ROW, REP), P(ROW, REP), P(REP, ROW, None))
    return jax.shard_map(local, mesh=fine, in_specs=in_specs, out_specs=out_specs, check_vma=False)
```

```python
import jax
import jax.numpy as jnp
from jax import lax
from jax.experimental import pallas as pl
from jax.experimental.pallas import tpu as pltpu
from jax.sharding import Mesh, PartitionSpec as P

outer_lr = 0.7
beta = 0.9

AXES = ("z", "x", "y", "c")
REP = ("z", "x")
ROW = ("y", "c")
ROUTES = (("x", "y", "z"), ("y", "z", "x"), ("z", "x", "y"))

HALF = 112
COUNTS = (37, 37, 38)
FIRST = (0, 37, 74)
BF = jnp.bfloat16
F32 = jnp.float32
HBM = pl.BlockSpec(memory_space=pltpu.HBM)
ANY = pl.BlockSpec(memory_space=pl.ANY)
VM = pl.BlockSpec(memory_space=pltpu.VMEM)
SM = pl.BlockSpec(memory_space=pltpu.SMEM)
DMA = pltpu.SemaphoreType.DMA


def params_of(mib=58):
    return pltpu.CompilerParams(vmem_limit_bytes=mib << 20)


def turn(x, axis, step):
    return lax.ppermute(x, axis, [(i, (i + step) % 4) for i in range(4)])


def low(x, axis):
    return lax.ppermute(x, axis, [(i, i ^ 1) for i in range(4)])


def high(x, axis):
    return lax.ppermute(x, axis, [(i, 3 - i) for i in range(4)])


def swap(x):
    return lax.ppermute(x, "c", [(0, 1), (1, 0)])


def start(src, dst, sem):
    copy = pltpu.make_async_copy(src, dst, sem)
    copy.start()
    return copy


P_BLOCK = 4096


def p_kernel(steps_ref, d_ref, e_ref, q_ref, out_ref, both_ref, qb_ref, sem):
    n = d_ref.shape[2] // P_BLOCK
    copies = []
    for i in range(n):
        cols = slice(i * P_BLOCK, (i + 1) * P_BLOCK)
        copies.append((
            start(d_ref.at[0, :, cols], both_ref.at[0:112, cols], sem.at[i, 0]),
            start(e_ref.at[0, :, cols], both_ref.at[112:224, cols], sem.at[i, 1]),
            start(q_ref.at[:, cols], qb_ref.at[:, cols], sem.at[i, 2]),
        ))
    acc_d = jnp.zeros((112, 64), F32)
    acc_e = jnp.zeros((112, 64), F32)
    dims = (((1,), (1,)), ((), ()))
    for i in range(n):
        cols = slice(i * P_BLOCK, (i + 1) * P_BLOCK)
        for copy in copies[i]:
            copy.wait()
        acc_d = acc_d + lax.dot_general(both_ref[0:112, cols], qb_ref[:, cols], dims, preferred_element_type=F32)
        acc_e = acc_e + lax.dot_general(both_ref[112:224, cols], qb_ref[:, cols], dims, preferred_element_type=F32)
    count = steps_ref[0].astype(F32)
    p = count * (acc_d + acc_e)
    out_ref[56:64, :] = jnp.full((8, 128), count, F32)
    out_ref[0:56, :] = jnp.concatenate([p[0:56], p[56:112]], axis=1)


def left_factor(delta, error, q_t, steps):
    width = delta.shape[2]
    return pl.pallas_call(
        p_kernel,
        in_specs=[SM, HBM, HBM, HBM],
        out_specs=VM,
        out_shape=jax.ShapeDtypeStruct((64, 128), F32),
        scratch_shapes=[
            pltpu.VMEM((224, width), BF),
            pltpu.VMEM((64, width), BF),
            DMA((width // P_BLOCK, 3)),
        ],
        compiler_params=params_of(),
        name="left_factor",
    )(steps, delta, error, q_t)


def prep_kernel(steps_ref, a_ref, b_ref, c_ref, d_ref, p_ref, lhs_ref, gram_ref):
    both = (a_ref[...] + b_ref[...]) + (c_ref[...] + d_ref[...])
    p = jnp.concatenate([both[0:56, 0:64], both[0:56, 64:128]], axis=0)
    total = both[56:57, 0:1]
    p_ref[...] = p
    top = jnp.max(jnp.abs(p), axis=0, keepdims=True)
    weight = steps_ref[0].astype(F32) / total
    unit = p * (1.0 / jnp.maximum(top, 1e-37)) * weight
    flat = unit.T
    upper = flat.astype(BF).astype(F32)
    rest = flat - upper
    lhs_ref[0:64, :] = jnp.concatenate([upper, upper], axis=1).astype(BF)
    lhs_ref[64:128, :] = jnp.concatenate([rest, rest], axis=1).astype(BF)
    gram_ref[...] = jnp.zeros_like(gram_ref)
    gram_ref[0:64, 0:64] = lax.dot_general(p, p, (((0,), (0,)), ((), ())), precision=lax.Precision.HIGHEST, preferred_element_type=F32)
    gram_ref[64:65, 0:64] = top


def prepare(steps, a, b, c, d):
    return pl.pallas_call(
        prep_kernel,
        in_specs=[SM, VM, VM, VM, VM],
        out_specs=[VM, VM, VM],
        out_shape=[
            jax.ShapeDtypeStruct((112, 64), F32),
            jax.ShapeDtypeStruct((128, 224), BF),
            jax.ShapeDtypeStruct((72, 128), F32),
        ],
        compiler_params=params_of(8),
        name="prepare",
    )(steps, a, b, c, d)


def blocks_of(tiles):
    return [(i, i + tiles) for i in range(0, HALF, tiles)]


def columns(side, begin, end):
    return pl.ds(pl.multiple_of(side * (HALF * 128) + begin * 128, 128), (end - begin) * 128)


def load_block(side, s, begin, end, d_ref, e_ref, both_ref, sem):
    src = columns(side, begin, end)
    return [
        start(d_ref.at[0, :, src], both_ref.at[s, 0:112, :], sem.at[s, 0]),
        start(e_ref.at[0, :, src], both_ref.at[s, 112:224, :], sem.at[s, 1]),
    ]


def chunk_range(k):
    return slice(FIRST[k], FIRST[k] + COUNTS[k])


def q_half(where, lhs, delta, error, far, *first):
    parts = blocks_of(28)
    n = len(parts)

    def kernel(s_ref, lhs_ref, d_ref, e_ref, *rest):
        rest = rest[len(first):]
        out_refs, (both_ref, sem), rest = rest[:3], rest[3:5], rest[5:]
        if far:
            v_ref, out_sem = rest
        side = 1 - s_ref[0] if far else s_ref[0]
        copies = [load_block(side, s, *parts[s], d_ref, e_ref, both_ref, sem) for s in range(n)]
        outs = []
        for s, (begin, end) in enumerate(parts):
            for copy in copies[s]:
                copy.wait()
            r = lax.dot_general(lhs_ref[...], both_ref[s], (((1,), (0,)), ((), ())), preferred_element_type=F32)
            v = r[0:64] + r[64:128]
            for t in range(begin, end):
                k = sum(t >= first for first in FIRST) - 1
                lanes = slice(128 * (t - begin), 128 * (t - begin) + 128)
                for i in range(8):
                    if far:
                        v_ref[i, t] = v[8 * i:8 * i + 8, lanes]
                    else:
                        out_refs[k][i, t - FIRST[k]] = v[8 * i:8 * i + 8, lanes]
            while far and len(outs) < 3 and FIRST[len(outs)] + COUNTS[len(outs)] <= end:
                k = len(outs)
                outs.append(start(v_ref.at[:, chunk_range(k)], out_refs[k], out_sem.at[k]))
        for copy in outs:
            copy.wait()

    return pl.pallas_call(
        kernel,
        in_specs=[SM, VM, HBM, HBM] + [ANY] * len(first),
        out_specs=[HBM if far else VM] * 3,
        out_shape=[jax.ShapeDtypeStruct((8, c, 8, 128), F32) for c in COUNTS],
        scratch_shapes=[
            pltpu.VMEM((n, 224, 28 * 128), BF),
            DMA((n, 2)),
        ] + [pltpu.VMEM((8, HALF, 8, 128), F32), DMA((3,))] * far,
        compiler_params=params_of(58 if far else 55),
        cost_estimate=pl.CostEstimate(flops=2 * 128 * 224 * HALF * 128, bytes_accessed=HALF * 128 * (448 + 256), transcendentals=0),
        name="q_far" if far else "q_own",
    )(where, lhs, delta, error, *first)


def blend(where, terms, arrived, f_own, f_near, gram):
    def kernel(s_ref, *refs):
        a_refs, b_refs, (f_ref, g_ref, gram_ref), refs = refs[:3], refs[3:6], refs[6:9], refs[9:]
        keep_refs, send_refs, (a_buf, b_buf, sem, out_sem) = refs[:3], refs[3:6], refs[6:]
        copies = []
        for k in range(3):
            copies.append((
                start(a_refs[k], a_buf.at[:, chunk_range(k)], sem.at[k, 0]),
                start(b_refs[k], b_buf.at[:, chunk_range(k)], sem.at[k, 1]),
            ))
        outs = []
        for k in range(3):
            for copy in copies[k]:
                copy.wait()
            tiles = chunk_range(k)
            for i in range(8):
                f = f_ref[8 * i:8 * i + 8, :][None]
                g = g_ref[8 * i:8 * i + 8, :][None]
                a_buf[i, tiles] = f * a_buf[i, tiles] + g * b_buf[i, tiles]
            bit = s_ref[1 + k]
            outs.append(start(a_buf.at[pl.ds(bit * 4, 4), tiles], keep_refs[k], out_sem.at[k, 4]))
            for i in range(4):
                place = slice(i * COUNTS[k], (i + 1) * COUNTS[k])
                outs.append(start(a_buf.at[(1 - bit) * 4 + i, tiles], send_refs[k].at[place], out_sem.at[k, i]))
            if ROUTES[k][0] == "y":
                outs.append(start(gram_ref, send_refs[k].at[slice(4 * COUNTS[k], 4 * COUNTS[k] + 9)], out_sem.at[k, 5]))
        for copy in outs:
            copy.wait()

    halves = [jax.ShapeDtypeStruct((4, c, 8, 128), F32) for c in COUNTS]
    away = [jax.ShapeDtypeStruct((4 * c + (9 if r[0] == "y" else 0), 8, 128), F32) for c, r in zip(COUNTS, ROUTES)]
    out = pl.pallas_call(
        kernel,
        in_specs=[SM] + [ANY] * 6 + [VM, VM, VM],
        out_specs=[HBM] * 6,
        out_shape=halves + away,
        scratch_shapes=[
            pltpu.VMEM((8, HALF, 8, 128), F32),
            pltpu.VMEM((8, HALF, 8, 128), F32),
            DMA((3, 2)),
            DMA((3, 6)),
        ],
        compiler_params=params_of(60),
        cost_estimate=pl.CostEstimate(flops=10 ** 6, bytes_accessed=11 * 10 ** 6, transcendentals=0),
        name="blend",
    )(where, *terms, *arrived, f_own, f_near, gram.reshape(9, 8, 128))
    return out[:3], out[3:]


def scales_kernel(a_ref, b_ref, *refs):
    sum_ref, f_a_ref, f_b_ref = refs[-3:]
    both = [ref[...] for ref in refs[:-3]]
    maxima = lax.broadcasted_iota(jnp.int32, (72, 128), 0) == 64
    while len(both) > 1:
        n = len(both) // 2
        both = [jnp.where(maxima, jnp.maximum(c, d), c + d) for c, d in zip(both[:n], both[n:])]
    both = both[0]
    sum_ref[...] = both
    eye = lax.broadcasted_iota(jnp.int32, (64, 64), 0) == lax.broadcasted_iota(jnp.int32, (64, 64), 1)
    top = jnp.maximum(both[64:65, 0:64], 1e-37)
    for src, dst in ((a_ref, f_a_ref), (b_ref, f_b_ref)):
        column = jnp.sum(jnp.where(eye, src[64:65, 0:64] / top, 0.0), axis=1, keepdims=True)
        dst[...] = jnp.broadcast_to(column, (64, 128))


def scales(a, b, *terms):
    both, f_a, f_b = pl.pallas_call(
        scales_kernel,
        in_specs=[VM] * (2 + len(terms)),
        out_specs=[VM] * 3,
        out_shape=[jax.ShapeDtypeStruct((72, 128), F32)] + [jax.ShapeDtypeStruct((64, 128), F32)] * 2,
        compiler_params=params_of(8),
        name="scales",
    )(a, b, *terms)
    return both, f_a, f_b


def solve_kernel(gram_ref, p_ref, block_ref, w_ref, block_out, sem):
    copy = start(block_ref, block_out, sem)
    highest = lax.Precision.HIGHEST
    row = lax.broadcasted_iota(jnp.int32, (64, 64), 0)
    lane = lax.broadcasted_iota(jnp.int32, (64, 64), 1)
    eye = (row == lane).astype(F32)
    inv_row = 1.0 / jnp.maximum(gram_ref[64:65, 0:64], 1e-37)
    inv_col = jnp.sum(eye * inv_row, axis=1, keepdims=True)
    unit = gram_ref[0:64, 0:64] * inv_col * inv_row
    m = jnp.concatenate([unit, eye], axis=1)
    below = lax.broadcasted_iota(jnp.int32, (64, 1), 0)
    for k in range(64):
        factor = jnp.where(below > k, m[:, k:k + 1], 0.0)
        m = m - factor * (m[k:k + 1, :] * (1.0 / m[k:k + 1, k:k + 1]))
    pivots = jnp.sum(eye * m[:, 0:64], axis=1, keepdims=True)
    inverse = m[:, 64:128] * (1.0 / jnp.sqrt(pivots))
    p_hat = lax.dot_general(p_ref[...] * inv_row, inverse, (((1,), (1,)), ((), ())), precision=highest, preferred_element_type=F32)
    w = lax.dot_general(p_hat, inverse, (((1,), (0,)), ((), ())), precision=highest, preferred_element_type=F32)
    upper = w.astype(BF).astype(F32)
    w_ref[...] = jnp.concatenate([upper, upper, w - upper], axis=1).astype(BF)
    copy.wait()


def solve(gram, p, block):
    return pl.pallas_call(
        solve_kernel,
        in_specs=[VM, VM, ANY],
        out_specs=[VM, HBM],
        out_shape=[jax.ShapeDtypeStruct((112, 192), BF), jax.ShapeDtypeStruct(block.shape, F32)],
        scratch_shapes=[DMA(())],
        compiler_params=params_of(8),
        cost_estimate=pl.CostEstimate(flops=10 ** 7, bytes_accessed=10 ** 7, transcendentals=0),
        name="solve",
    )(gram, p, block)


def finish(where, w, sides, delta, error, params, momentum, base, far):
    parts = blocks_of(14)
    n = len(parts)
    wide = 14 * 128
    given = len(base)

    def kernel(s_ref, w_ref, *rest):
        q_refs, (d_ref, e_ref, par_ref, mom_ref), rest = rest[:6], rest[6:10], rest[10 + given:]
        err_ref, np_ref, nm_ref, both_ref, q_ref, new_ref, pb_ref, mb_ref, po_ref, mo_ref, sem, q_sem, out_sem, par_sem = rest
        side = 1 - s_ref[0] if far else s_ref[0]
        turn_of = s_ref[4] - 8 * side
        mine = (turn_of >= 0) & (turn_of < 8)

        q_copies, copies = [], []
        for s in range(n):
            copies.append(load_block(side, s, *parts[s], d_ref, e_ref, both_ref, sem))
            k = len(q_copies)
            if k < 3 and s % 2 == 0:
                bit = s_ref[1 + k]
                q_copies.append([
                    start(q_refs[2 * k], q_ref.at[pl.ds(bit * 4, 4), chunk_range(k)], q_sem.at[k, 0]),
                    start(q_refs[2 * k + 1], q_ref.at[pl.ds((1 - bit) * 4, 4), chunk_range(k)], q_sem.at[k, 1]),
                ])

        @pl.when(mine)
        def _():
            start(par_ref, pb_ref, par_sem.at[0])
            start(mom_ref, mb_ref, par_sem.at[1])

        outs = []
        for s, (begin, end) in enumerate(parts):
            while q_copies and FIRST[3 - len(q_copies)] < end:
                for copy in q_copies.pop(0):
                    copy.wait()
            for copy in copies[s]:
                copy.wait()
            q = jnp.concatenate([jnp.concatenate([q_ref[i, t] for t in range(begin, end)], axis=1) for i in range(8)], axis=0)
            upper = q.astype(BF)
            below = (q - upper.astype(F32)).astype(BF)
            rhs = jnp.concatenate([upper, below, upper], axis=0)
            approx = lax.dot_general(w_ref[...], rhs, (((1,), (0,)), ((), ())), preferred_element_type=F32)
            merged = both_ref[s, 0:112, :].astype(F32) + both_ref[s, 112:224, :].astype(F32)
            new_ref[s] = (merged - approx).astype(BF)
            outs.append(start(new_ref.at[s], err_ref.at[0, :, columns(side, begin, end)], out_sem.at[s]))

            @pl.when(turn_of == s)
            def _():
                pltpu.make_async_copy(par_ref, pb_ref, par_sem.at[0]).wait()
                pltpu.make_async_copy(mom_ref, mb_ref, par_sem.at[1]).wait()
                fresh = beta * mb_ref[...] + approx
                mo_ref[...] = fresh
                po_ref[...] = pb_ref[...] - outer_lr * (approx + beta * fresh)
                start(po_ref, np_ref, par_sem.at[2])
                start(mo_ref, nm_ref, par_sem.at[3])

        for copy in outs:
            copy.wait()

        @pl.when(mine)
        def _():
            pltpu.make_async_copy(po_ref, np_ref, par_sem.at[2]).wait()
            pltpu.make_async_copy(mo_ref, nm_ref, par_sem.at[3]).wait()

    panel = pltpu.VMEM((112, wide), F32)
    return pl.pallas_call(
        kernel,
        in_specs=[SM, VM] + [ANY] * 6 + [HBM] * (4 + given),
        out_specs=[HBM, HBM, HBM],
        out_shape=[
            jax.ShapeDtypeStruct(delta.shape, BF),
            jax.ShapeDtypeStruct(params.shape, F32),
            jax.ShapeDtypeStruct(params.shape, F32),
        ],
        input_output_aliases={12 + i: i for i in range(given)},
        scratch_shapes=[
            pltpu.VMEM((n, 224, wide), BF),
            pltpu.VMEM((8, HALF, 8, 128), F32),
            pltpu.VMEM((n, 112, wide), BF),
            panel, panel, panel, panel,
            DMA((n, 2)),
            DMA((3, 2)),
            DMA((n,)),
            DMA((4,)),
        ],
        compiler_params=params_of(),
        cost_estimate=pl.CostEstimate(flops=2 * 112 * 192 * HALF * 128, bytes_accessed=HALF * 128 * (672 + 256), transcendentals=0),
        name="finish_far" if far else "finish_own",
    )(where, w, *sides, delta, error, params, momentum, *base)


def local(delta, error, steps, q_start, params, momentum):
    place = {a: lax.axis_index(a) for a in AXES}
    core = place["c"]
    hi_bit = {a: place[a] // 2 for a in REP + ("y",)}
    lo_bit = {a: (place[a] + place[a] // 2) % 2 for a in REP + ("y",)}
    where = jnp.stack([core] + [lo_bit[r[0]] for r in ROUTES] + [lax.axis_index(REP)])

    own = left_factor(delta, error, q_start.T, steps)
    own = (own + turn(own, "x", 2)) + (turn(own, "x", 1) + turn(own, "x", 3))
    p_all, lhs, gram_own = prepare(steps, own, turn(own, "z", 2), turn(own, "z", 1), turn(own, "z", 3))

    gram_near = swap(gram_own)
    chip, f_own, f_near = scales(gram_own, gram_near, gram_own, gram_near)

    arrived = [swap(v) for v in q_half(where, lhs, delta, error, True)]
    terms = q_half(where, lhs, delta, error, False)
    keeps, sends = blend(where, terms, arrived, f_own, f_near, chip)
    half = lambda x, b: lax.dynamic_slice_in_dim(x, b * (x.shape[0] // 2), x.shape[0] // 2, 0)
    gots = [low(send, route[0]) for send, route in zip(sends, ROUTES)]
    rest = 4 * COUNTS[1]
    chip_near = gots[1][rest:].reshape(72, 128)
    gots = [got[:4 * c].reshape(4, c, 8, 128) for got, c in zip(gots, COUNTS)]
    pair, g_own, g_near = scales(chip, chip_near, chip, chip_near)
    parts = []
    for k, route in enumerate(ROUTES):
        keep, got = keeps[k], gots[k]
        ours, theirs = [g.reshape(8, 1, 8, 128) for g in (g_own, g_near)]
        for step in range(3):
            ours, theirs = [half(g, lo_bit[route[step]]) for g in (ours, theirs)]
            scaled = route[step] == "y"
            if step == 2:
                parts.append(keep[0] * ours[0] + got[0] * theirs[0] if scaled else keep[0] + got[0])
                break
            bit = lo_bit[route[step + 1]]

            def take(b):
                if scaled:
                    return half(keep, b) * half(ours, b) + half(got, b) * half(theirs, b)
                return half(keep, b) + half(got, b)

            send, keep = take(1 - bit), take(bit)
            got = low(send, route[step + 1])
    mine = jnp.concatenate(parts, axis=0)
    got = high(jnp.concatenate([half(mine, 1 - hi_bit["y"]), pair.reshape(9, 8, 128)], axis=0), "y")
    pair_near = got[56:].reshape(72, 128)
    both, h_own, h_near = scales(pair, pair_near, pair, pair_near)

    def per_tile(h):
        rows = h.reshape(8, 8, 128)
        spread = []
        for k, route in enumerate(ROUTES):
            block = sum(lo_bit[d] * (4 >> i) for i, d in enumerate(route))
            spread.append(jnp.broadcast_to(lax.dynamic_slice_in_dim(rows, block, 1, 0), (COUNTS[k], 8, 128)))
        return half(jnp.concatenate(spread, axis=0), hi_bit["y"])

    mine = half(mine, hi_bit["y"]) * per_tile(h_own) + got[:56] * per_tile(h_near)
    quarter = lambda a, b: lax.dynamic_slice_in_dim(mine, (2 * a + b) * 14, 14, 0)
    hz, hx = hi_bit["z"], hi_bit["x"]
    both_high = lambda x: lax.ppermute(x, REP, [(4 * i + j, 4 * (3 - i) + 3 - j) for i in range(4) for j in range(4)])
    mine = (quarter(hz, hx) + both_high(quarter(1 - hz, 1 - hx))) + (high(quarter(1 - hz, hx), "z") + high(quarter(hz, 1 - hx), "x"))

    def in_order(bit, a, b):
        return jnp.where(bit == 0, jnp.concatenate([a, b], 0), jnp.concatenate([b, a], 0))

    across = {0: mine, 1: high(mine, "x"), 2: high(mine, "z"), 3: both_high(mine)}
    by_x = [in_order(hx, across[m], across[m + 1]) for m in (0, 2)]
    mine = in_order(hz, *by_x)
    mine = in_order(hi_bit["y"], mine, high(mine, "y"))
    sides = []
    for k, route in enumerate(ROUTES):
        v = mine[chunk_range(k)][None]
        for d in route[:0:-1]:
            v = in_order(lo_bit[d], v, low(v, d))
        sides.append((v, low(v, route[0])))
    w_cat, last = solve(both, p_all, sides[2][0])
    far = [swap(x) for pair in sides[:2] for x in pair] + [swap(last), swap(sides[2][1])]
    near = [x for pair in sides for x in pair]
    base = finish(where, w_cat, near, delta, error, params, momentum, (), False)
    base = finish(where, w_cat, far, delta, error, params, momentum, base, True)
    error_new, params_new, momentum_new = base
    return (params_new, momentum_new, error_new)


def solution(mesh):
    fine = Mesh(mesh.devices.reshape(4, 4, 4, 2), AXES)
    in_specs = (
        P(REP, ROW, None),
        P(REP, ROW, None),
        P(REP),
        P(),
        P(ROW, REP),
        P(ROW, REP),
    )
    out_specs = (P(ROW, REP), P(ROW, REP), P(REP, ROW, None))
    return jax.shard_map(local, mesh=fine, in_specs=in_specs, out_specs=out_specs, check_vma=False)
```

```python
import jax
import jax.numpy as jnp
from jax import lax
from jax.experimental import pallas as pl
from jax.experimental.pallas import tpu as pltpu
from jax.sharding import Mesh, PartitionSpec as P

outer_lr = 0.7
beta = 0.9

AXES = ("z", "x", "y", "c")
REP = ("z", "x")
ROW = ("y", "c")
ROUTES = (("x", "y", "z"), ("y", "z", "x"), ("z", "x", "y"))

HALF = 112
COUNTS = (38, 36, 38)
FIRST = (0, 38, 74)
BF = jnp.bfloat16
F32 = jnp.float32
HBM = pl.BlockSpec(memory_space=pltpu.HBM)
ANY = pl.BlockSpec(memory_space=pl.ANY)
VM = pl.BlockSpec(memory_space=pltpu.VMEM)
SM = pl.BlockSpec(memory_space=pltpu.SMEM)
DMA = pltpu.SemaphoreType.DMA


def params_of(mib=58):
    return pltpu.CompilerParams(vmem_limit_bytes=mib << 20)


def turn(x, axis, step):
    return lax.ppermute(x, axis, [(i, (i + step) % 4) for i in range(4)])


def low(x, axis):
    return lax.ppermute(x, axis, [(i, i ^ 1) for i in range(4)])


def high(x, axis):
    return lax.ppermute(x, axis, [(i, 3 - i) for i in range(4)])


def swap(x):
    return lax.ppermute(x, "c", [(0, 1), (1, 0)])


def start(src, dst, sem):
    copy = pltpu.make_async_copy(src, dst, sem)
    copy.start()
    return copy


P_BLOCK = 4096


def p_kernel(steps_ref, d_ref, e_ref, q_ref, out_ref, both_ref, qb_ref, sem):
    n = d_ref.shape[2] // P_BLOCK
    copies = []
    for i in range(n):
        cols = slice(i * P_BLOCK, (i + 1) * P_BLOCK)
        copies.append((
            start(d_ref.at[0, :, cols], both_ref.at[0:112, cols], sem.at[i, 0]),
            start(e_ref.at[0, :, cols], both_ref.at[112:224, cols], sem.at[i, 1]),
            start(q_ref.at[:, cols], qb_ref.at[:, cols], sem.at[i, 2]),
        ))
    acc_d = jnp.zeros((112, 64), F32)
    acc_e = jnp.zeros((112, 64), F32)
    dims = (((1,), (1,)), ((), ()))
    for i in range(n):
        cols = slice(i * P_BLOCK, (i + 1) * P_BLOCK)
        for copy in copies[i]:
            copy.wait()
        acc_d = acc_d + lax.dot_general(both_ref[0:112, cols], qb_ref[:, cols], dims, preferred_element_type=F32)
        acc_e = acc_e + lax.dot_general(both_ref[112:224, cols], qb_ref[:, cols], dims, preferred_element_type=F32)
    count = steps_ref[0].astype(F32)
    p = count * (acc_d + acc_e)
    out_ref[56:64, :] = jnp.full((8, 128), count, F32)
    out_ref[0:56, :] = jnp.concatenate([p[0:56], p[56:112]], axis=1)


def left_factor(delta, error, q_t, steps):
    width = delta.shape[2]
    return pl.pallas_call(
        p_kernel,
        in_specs=[SM, HBM, HBM, HBM],
        out_specs=VM,
        out_shape=jax.ShapeDtypeStruct((64, 128), F32),
        scratch_shapes=[
            pltpu.VMEM((224, width), BF),
            pltpu.VMEM((64, width), BF),
            DMA((width // P_BLOCK, 3)),
        ],
        compiler_params=params_of(),
        name="left_factor",
    )(steps, delta, error, q_t)


def prep_kernel(steps_ref, a_ref, b_ref, c_ref, d_ref, p_ref, lhs_ref, gram_ref):
    both = (a_ref[...] + b_ref[...]) + (c_ref[...] + d_ref[...])
    p = jnp.concatenate([both[0:56, 0:64], both[0:56, 64:128]], axis=0)
    total = both[56:57, 0:1]
    p_ref[...] = p
    top = jnp.max(jnp.abs(p), axis=0, keepdims=True)
    weight = steps_ref[0].astype(F32) / total
    unit = p * (1.0 / jnp.maximum(top, 1e-37)) * weight
    flat = unit.T
    upper = flat.astype(BF).astype(F32)
    rest = flat - upper
    lhs_ref[0:64, :] = jnp.concatenate([upper, upper], axis=1).astype(BF)
    lhs_ref[64:128, :] = jnp.concatenate([rest, rest], axis=1).astype(BF)
    gram_ref[...] = jnp.zeros_like(gram_ref)
    gram_ref[0:64, 0:64] = lax.dot_general(p, p, (((0,), (0,)), ((), ())), precision=lax.Precision.HIGHEST, preferred_element_type=F32)
    gram_ref[64:65, 0:64] = top


def prepare(steps, a, b, c, d):
    return pl.pallas_call(
        prep_kernel,
        in_specs=[SM, VM, VM, VM, VM],
        out_specs=[VM, VM, VM],
        out_shape=[
            jax.ShapeDtypeStruct((112, 64), F32),
            jax.ShapeDtypeStruct((128, 224), BF),
            jax.ShapeDtypeStruct((72, 128), F32),
        ],
        compiler_params=params_of(8),
        name="prepare",
    )(steps, a, b, c, d)


def blocks_of(tiles):
    return [(i, i + tiles) for i in range(0, HALF, tiles)]


def columns(side, begin, end):
    return pl.ds(pl.multiple_of(side * (HALF * 128) + begin * 128, 128), (end - begin) * 128)


def load_block(side, s, begin, end, d_ref, e_ref, both_ref, sem):
    src = columns(side, begin, end)
    return [
        start(d_ref.at[0, :, src], both_ref.at[s, 0:112, :], sem.at[s, 0]),
        start(e_ref.at[0, :, src], both_ref.at[s, 112:224, :], sem.at[s, 1]),
    ]


def chunk_range(k):
    return slice(FIRST[k], FIRST[k] + COUNTS[k])


def q_half(where, lhs, delta, error, far, *first):
    parts = blocks_of(28)
    n = len(parts)

    def kernel(s_ref, lhs_ref, d_ref, e_ref, *rest):
        rest = rest[len(first):]
        out_refs, (both_ref, v_ref, sem, out_sem) = rest[:3], rest[3:]
        side = 1 - s_ref[0] if far else s_ref[0]
        copies = [load_block(side, s, *parts[s], d_ref, e_ref, both_ref, sem) for s in range(n)]
        outs = []
        for s, (begin, end) in enumerate(parts):
            for copy in copies[s]:
                copy.wait()
            r = lax.dot_general(lhs_ref[...], both_ref[s], (((1,), (0,)), ((), ())), preferred_element_type=F32)
            v = r[0:64] + r[64:128]
            for i in range(8):
                for t in range(end - begin):
                    v_ref[i, begin + t] = v[8 * i:8 * i + 8, 128 * t:128 * t + 128]
            while len(outs) < 3 and FIRST[len(outs)] + COUNTS[len(outs)] <= end:
                k = len(outs)
                outs.append(start(v_ref.at[:, chunk_range(k)], out_refs[k], out_sem.at[k]))
        for copy in outs:
            copy.wait()

    return pl.pallas_call(
        kernel,
        in_specs=[SM, VM, HBM, HBM] + [ANY] * len(first),
        out_specs=[HBM] * 3,
        out_shape=[jax.ShapeDtypeStruct((8, c, 8, 128), F32) for c in COUNTS],
        scratch_shapes=[
            pltpu.VMEM((n, 224, 28 * 128), BF),
            pltpu.VMEM((8, HALF, 8, 128), F32),
            DMA((n, 2)),
            DMA((3,)),
        ],
        compiler_params=params_of(),
        cost_estimate=pl.CostEstimate(flops=2 * 128 * 224 * HALF * 128, bytes_accessed=HALF * 128 * (448 + 256), transcendentals=0),
        name="q_far" if far else "q_own",
    )(where, lhs, delta, error, *first)


def blend(where, terms, arrived, f_own, f_near, gram):
    def kernel(s_ref, *refs):
        a_refs, b_refs, (f_ref, g_ref, gram_ref), refs = refs[:3], refs[3:6], refs[6:9], refs[9:]
        keep_refs, send_refs, (a_buf, b_buf, sem, out_sem) = refs[:3], refs[3:6], refs[6:]
        copies = []
        for k in range(3):
            copies.append((
                start(a_refs[k], a_buf.at[:, chunk_range(k)], sem.at[k, 0]),
                start(b_refs[k], b_buf.at[:, chunk_range(k)], sem.at[k, 1]),
            ))
        outs = []
        for k in range(3):
            for copy in copies[k]:
                copy.wait()
            tiles = chunk_range(k)
            for i in range(8):
                f = f_ref[8 * i:8 * i + 8, :][None]
                g = g_ref[8 * i:8 * i + 8, :][None]
                a_buf[i, tiles] = f * a_buf[i, tiles] + g * b_buf[i, tiles]
            bit = s_ref[1 + k]
            outs.append(start(a_buf.at[pl.ds(bit * 4, 4), tiles], keep_refs[k], out_sem.at[k, 4]))
            for i in range(4):
                place = slice(i * COUNTS[k], (i + 1) * COUNTS[k])
                outs.append(start(a_buf.at[(1 - bit) * 4 + i, tiles], send_refs[k].at[place], out_sem.at[k, i]))
            if ROUTES[k][0] == "y":
                outs.append(start(gram_ref, send_refs[k].at[slice(4 * COUNTS[k], 4 * COUNTS[k] + 9)], out_sem.at[k, 5]))
        for copy in outs:
            copy.wait()

    halves = [jax.ShapeDtypeStruct((4, c, 8, 128), F32) for c in COUNTS]
    away = [jax.ShapeDtypeStruct((4 * c + (9 if r[0] == "y" else 0), 8, 128), F32) for c, r in zip(COUNTS, ROUTES)]
    out = pl.pallas_call(
        kernel,
        in_specs=[SM] + [ANY] * 6 + [VM, VM, VM],
        out_specs=[HBM] * 6,
        out_shape=halves + away,
        scratch_shapes=[
            pltpu.VMEM((8, HALF, 8, 128), F32),
            pltpu.VMEM((8, HALF, 8, 128), F32),
            DMA((3, 2)),
            DMA((3, 6)),
        ],
        compiler_params=params_of(16),
        cost_estimate=pl.CostEstimate(flops=10 ** 6, bytes_accessed=11 * 10 ** 6, transcendentals=0),
        name="blend",
    )(where, *terms, *arrived, f_own, f_near, gram.reshape(9, 8, 128))
    return out[:3], out[3:]


def scales_kernel(a_ref, b_ref, *refs):
    sum_ref, f_a_ref, f_b_ref = refs[-3:]
    both = [ref[...] for ref in refs[:-3]]
    maxima = lax.broadcasted_iota(jnp.int32, (72, 128), 0) == 64
    while len(both) > 1:
        n = len(both) // 2
        both = [jnp.where(maxima, jnp.maximum(c, d), c + d) for c, d in zip(both[:n], both[n:])]
    both = both[0]
    sum_ref[...] = both
    eye = lax.broadcasted_iota(jnp.int32, (64, 64), 0) == lax.broadcasted_iota(jnp.int32, (64, 64), 1)
    top = jnp.maximum(both[64:65, 0:64], 1e-37)
    for src, dst in ((a_ref, f_a_ref), (b_ref, f_b_ref)):
        column = jnp.sum(jnp.where(eye, src[64:65, 0:64] / top, 0.0), axis=1, keepdims=True)
        dst[...] = jnp.broadcast_to(column, (64, 128))


def scales(a, b, *terms):
    both, f_a, f_b = pl.pallas_call(
        scales_kernel,
        in_specs=[VM] * (2 + len(terms)),
        out_specs=[VM] * 3,
        out_shape=[jax.ShapeDtypeStruct((72, 128), F32)] + [jax.ShapeDtypeStruct((64, 128), F32)] * 2,
        compiler_params=params_of(8),
        name="scales",
    )(a, b, *terms)
    return both, f_a, f_b


def solve_kernel(gram_ref, p_ref, block_ref, w_ref, block_out, sem):
    copy = start(block_ref, block_out, sem)
    highest = lax.Precision.HIGHEST
    row = lax.broadcasted_iota(jnp.int32, (64, 64), 0)
    lane = lax.broadcasted_iota(jnp.int32, (64, 64), 1)
    eye = (row == lane).astype(F32)
    inv_row = 1.0 / jnp.maximum(gram_ref[64:65, 0:64], 1e-37)
    inv_col = jnp.sum(eye * inv_row, axis=1, keepdims=True)
    unit = gram_ref[0:64, 0:64] * inv_col * inv_row
    m = jnp.concatenate([unit, eye], axis=1)
    below = lax.broadcasted_iota(jnp.int32, (64, 1), 0)
    for k in range(64):
        factor = jnp.where(below > k, m[:, k:k + 1], 0.0)
        m = m - factor * (m[k:k + 1, :] * (1.0 / m[k:k + 1, k:k + 1]))
    pivots = jnp.sum(eye * m[:, 0:64], axis=1, keepdims=True)
    inverse = m[:, 64:128] * (1.0 / jnp.sqrt(pivots))
    p_hat = lax.dot_general(p_ref[...] * inv_row, inverse, (((1,), (1,)), ((), ())), precision=highest, preferred_element_type=F32)
    w = lax.dot_general(p_hat, inverse, (((1,), (0,)), ((), ())), precision=highest, preferred_element_type=F32)
    upper = w.astype(BF).astype(F32)
    w_ref[...] = jnp.concatenate([upper, upper, w - upper], axis=1).astype(BF)
    copy.wait()


def solve(gram, p, block):
    return pl.pallas_call(
        solve_kernel,
        in_specs=[VM, VM, ANY],
        out_specs=[VM, HBM],
        out_shape=[jax.ShapeDtypeStruct((112, 192), BF), jax.ShapeDtypeStruct(block.shape, F32)],
        scratch_shapes=[DMA(())],
        compiler_params=params_of(8),
        cost_estimate=pl.CostEstimate(flops=10 ** 7, bytes_accessed=10 ** 7, transcendentals=0),
        name="solve",
    )(gram, p, block)


def finish(where, w, sides, delta, error, params, momentum, base, far):
    parts = blocks_of(14)
    n = len(parts)
    wide = 14 * 128
    given = len(base)

    def kernel(s_ref, w_ref, *rest):
        q_refs, (d_ref, e_ref, par_ref, mom_ref), rest = rest[:6], rest[6:10], rest[10 + given:]
        err_ref, np_ref, nm_ref, both_ref, q_ref, new_ref, pb_ref, mb_ref, po_ref, mo_ref, sem, q_sem, out_sem, par_sem = rest
        side = 1 - s_ref[0] if far else s_ref[0]
        turn_of = s_ref[4] - 8 * side
        mine = (turn_of >= 0) & (turn_of < 8)

        q_copies, copies = [], []
        for s in range(n):
            copies.append(load_block(side, s, *parts[s], d_ref, e_ref, both_ref, sem))
            k = len(q_copies)
            if k < 3 and s % 2 == 0:
                bit = s_ref[1 + k]
                q_copies.append([
                    start(q_refs[2 * k], q_ref.at[pl.ds(bit * 4, 4), chunk_range(k)], q_sem.at[k, 0]),
                    start(q_refs[2 * k + 1], q_ref.at[pl.ds((1 - bit) * 4, 4), chunk_range(k)], q_sem.at[k, 1]),
                ])

        @pl.when(mine)
        def _():
            start(par_ref, pb_ref, par_sem.at[0])
            start(mom_ref, mb_ref, par_sem.at[1])

        outs = []
        for s, (begin, end) in enumerate(parts):
            while q_copies and FIRST[3 - len(q_copies)] < end:
                for copy in q_copies.pop(0):
                    copy.wait()
            for copy in copies[s]:
                copy.wait()
            q = jnp.concatenate([jnp.concatenate([q_ref[i, t] for t in range(begin, end)], axis=1) for i in range(8)], axis=0)
            upper = q.astype(BF)
            below = (q - upper.astype(F32)).astype(BF)
            rhs = jnp.concatenate([upper, below, upper], axis=0)
            approx = lax.dot_general(w_ref[...], rhs, (((1,), (0,)), ((), ())), preferred_element_type=F32)
            merged = both_ref[s, 0:112, :].astype(F32) + both_ref[s, 112:224, :].astype(F32)
            new_ref[s] = (merged - approx).astype(BF)
            outs.append(start(new_ref.at[s], err_ref.at[0, :, columns(side, begin, end)], out_sem.at[s]))

            @pl.when(turn_of == s)
            def _():
                pltpu.make_async_copy(par_ref, pb_ref, par_sem.at[0]).wait()
                pltpu.make_async_copy(mom_ref, mb_ref, par_sem.at[1]).wait()
                fresh = beta * mb_ref[...] + approx
                mo_ref[...] = fresh
                po_ref[...] = pb_ref[...] - outer_lr * (approx + beta * fresh)
                start(po_ref, np_ref, par_sem.at[2])
                start(mo_ref, nm_ref, par_sem.at[3])

        for copy in outs:
            copy.wait()

        @pl.when(mine)
        def _():
            pltpu.make_async_copy(po_ref, np_ref, par_sem.at[2]).wait()
            pltpu.make_async_copy(mo_ref, nm_ref, par_sem.at[3]).wait()

    panel = pltpu.VMEM((112, wide), F32)
    return pl.pallas_call(
        kernel,
        in_specs=[SM, VM] + [ANY] * 6 + [HBM] * (4 + given),
        out_specs=[HBM, HBM, HBM],
        out_shape=[
            jax.ShapeDtypeStruct(delta.shape, BF),
            jax.ShapeDtypeStruct(params.shape, F32),
            jax.ShapeDtypeStruct(params.shape, F32),
        ],
        input_output_aliases={12 + i: i for i in range(given)},
        scratch_shapes=[
            pltpu.VMEM((n, 224, wide), BF),
            pltpu.VMEM((8, HALF, 8, 128), F32),
            pltpu.VMEM((n, 112, wide), BF),
            panel, panel, panel, panel,
            DMA((n, 2)),
            DMA((3, 2)),
            DMA((n,)),
            DMA((4,)),
        ],
        compiler_params=params_of(),
        cost_estimate=pl.CostEstimate(flops=2 * 112 * 192 * HALF * 128, bytes_accessed=HALF * 128 * (672 + 256), transcendentals=0),
        name="finish_far" if far else "finish_own",
    )(where, w, *sides, delta, error, params, momentum, *base)


def local(delta, error, steps, q_start, params, momentum):
    place = {a: lax.axis_index(a) for a in AXES}
    core = place["c"]
    hi_bit = {a: place[a] // 2 for a in REP + ("y",)}
    lo_bit = {a: (place[a] + place[a] // 2) % 2 for a in REP + ("y",)}
    where = jnp.stack([core] + [lo_bit[r[0]] for r in ROUTES] + [lax.axis_index(REP)])

    own = left_factor(delta, error, q_start.T, steps)
    own = (own + turn(own, "x", 2)) + (turn(own, "x", 1) + turn(own, "x", 3))
    p_all, lhs, gram_own = prepare(steps, own, turn(own, "z", 2), turn(own, "z", 1), turn(own, "z", 3))

    gram_near = swap(gram_own)
    chip, f_own, f_near = scales(gram_own, gram_near, gram_own, gram_near)

    arrived = [swap(v) for v in q_half(where, lhs, delta, error, True)]
    terms = q_half(where, lhs, delta, error, False)
    keeps, sends = blend(where, terms, arrived, f_own, f_near, chip)
    half = lambda x, b: lax.dynamic_slice_in_dim(x, b * (x.shape[0] // 2), x.shape[0] // 2, 0)
    gots = [low(send, route[0]) for send, route in zip(sends, ROUTES)]
    rest = 4 * COUNTS[1]
    chip_near = gots[1][rest:].reshape(72, 128)
    gots = [got[:4 * c].reshape(4, c, 8, 128) for got, c in zip(gots, COUNTS)]
    pair, g_own, g_near = scales(chip, chip_near, chip, chip_near)
    parts = []
    for k, route in enumerate(ROUTES):
        keep, got = keeps[k], gots[k]
        ours, theirs = [g.reshape(8, 1, 8, 128) for g in (g_own, g_near)]
        for step in range(3):
            ours, theirs = [half(g, lo_bit[route[step]]) for g in (ours, theirs)]
            scaled = route[step] == "y"
            if step == 2:
                parts.append(keep[0] * ours[0] + got[0] * theirs[0] if scaled else keep[0] + got[0])
                break
            bit = lo_bit[route[step + 1]]

            def take(b):
                if scaled:
                    return half(keep, b) * half(ours, b) + half(got, b) * half(theirs, b)
                return half(keep, b) + half(got, b)

            send, keep = take(1 - bit), take(bit)
            got = low(send, route[step + 1])
    mine = jnp.concatenate(parts, axis=0)
    got = high(jnp.concatenate([half(mine, 1 - hi_bit["y"]), pair.reshape(9, 8, 128)], axis=0), "y")
    pair_near = got[56:].reshape(72, 128)
    both, h_own, h_near = scales(pair, pair_near, pair, pair_near)

    def per_tile(h):
        rows = h.reshape(8, 8, 128)
        spread = []
        for k, route in enumerate(ROUTES):
            block = sum(lo_bit[d] * (4 >> i) for i, d in enumerate(route))
            spread.append(jnp.broadcast_to(lax.dynamic_slice_in_dim(rows, block, 1, 0), (COUNTS[k], 8, 128)))
        return half(jnp.concatenate(spread, axis=0), hi_bit["y"])

    mine = half(mine, hi_bit["y"]) * per_tile(h_own) + got[:56] * per_tile(h_near)
    quarter = lambda a, b: lax.dynamic_slice_in_dim(mine, (2 * a + b) * 14, 14, 0)
    hz, hx = hi_bit["z"], hi_bit["x"]
    both_high = lambda x: lax.ppermute(x, REP, [(4 * i + j, 4 * (3 - i) + 3 - j) for i in range(4) for j in range(4)])
    mine = (quarter(hz, hx) + both_high(quarter(1 - hz, 1 - hx))) + (high(quarter(1 - hz, hx), "z") + high(quarter(hz, 1 - hx), "x"))

    def in_order(bit, a, b):
        return jnp.where(bit == 0, jnp.concatenate([a, b], 0), jnp.concatenate([b, a], 0))

    across = {0: mine, 1: high(mine, "x"), 2: high(mine, "z"), 3: both_high(mine)}
    by_x = [in_order(hx, across[m], across[m + 1]) for m in (0, 2)]
    mine = in_order(hz, *by_x)
    mine = in_order(hi_bit["y"], mine, high(mine, "y"))
    sides = []
    for k, route in enumerate(ROUTES):
        v = mine[chunk_range(k)][None]
        for d in route[:0:-1]:
            v = in_order(lo_bit[d], v, low(v, d))
        sides.append((v, low(v, route[0])))
    w_cat, last = solve(both, p_all, sides[2][0])
    far = [swap(x) for pair in sides[:2] for x in pair] + [swap(last), swap(sides[2][1])]
    near = [x for pair in sides for x in pair]
    base = finish(where, w_cat, near, delta, error, params, momentum, (), False)
    base = finish(where, w_cat, far, delta, error, params, momentum, base, True)
    error_new, params_new, momentum_new = base
    return (params_new, momentum_new, error_new)


def solution(mesh):
    fine = Mesh(mesh.devices.reshape(4, 4, 4, 2), AXES)
    in_specs = (
        P(REP, ROW, None),
        P(REP, ROW, None),
        P(REP),
        P(),
        P(ROW, REP),
        P(ROW, REP),
    )
    out_specs = (P(ROW, REP), P(ROW, REP), P(REP, ROW, None))
    return jax.shard_map(local, mesh=fine, in_specs=in_specs, out_specs=out_specs, check_vma=False)
```
